32 devices in a mesh: groups: 2 (over y), dp: 4 (over z), tensor: 2 (over x), seq: 2 (over core).
Axes of the slice: x: 2, y: 2, z: 4, core: 2. Of those that a mesh axis runs over, the one named last changes fastest.
Arguments:
- cache: bfloat16 [8, 2, 8, 256, 1024], P(('groups', 'dp'), None, 'seq', None, 'tensor'), parts along dimension 0, may hold values from -6 to 6
- query: bfloat16 [8, 2, 8192], P(('groups', 'dp'), None, 'tensor'), parts along dimension 0
- fresh_key_values: bfloat16 [8, 2, 2, 1024], P(('groups', 'dp'), None, None, 'tensor'), parts along dimension 0, may hold values from -6 to 6
- parents: int32 [8], P('groups'), parts along dimension 0, may hold values from 0 to 3
- lengths: int32 [8], P('groups'), parts along dimension 0, may hold values from 512 to 2048
- page_table: int32 [8, 8], P('groups'), parts along dimension 0, may hold values from 0 to 7, as said below
- out_weight: bfloat16 [8192, 8192], P('tensor', ('dp', 'seq')), may hold values from -0.0625 to 0.0625
Outputs:
- moved_cache: bfloat16 [8, 2, 8, 256, 1024], P(('groups', 'dp'), None, 'seq', None, 'tensor'), parts along dimension 0
- projected: bfloat16 [16, 8192], P(('groups', 'tensor'), ('dp', 'seq')), parts along dimension 0
The draws below stay inside these ranges and needn't reach their ends.
There are 2 independent parts, one for each index of `groups`. The reference program is written for one: setup_inputs(seed, part) draws one part's arguments, and reference() takes and returns one part's arrays. A program takes and returns all parts, laid end to end along the dimension named above; an argument that names none is the same for every part. Nothing has to cross between parts.
Inputs may be any that keep to these rules, and one draw needn't show every extreme that they name: `page_table`: every row is a permutation of the storage slots 0 to 7.
All inputs are finite; a program needn't handle non-finite values.
Results may differ from the reference program's by a relative error of at most 0.009.
Values may be sent and summed in bfloat16 or wider, within the bound.
A program may use at most 64 MiB of HBM per device.

```python
import math
import jax
import jax.numpy as jnp
import numpy as np
from jax import lax

D = 8192
QUERY_HEADS = 64
KEY_VALUE_HEADS = 8
HEAD_SIZE = 128
PAGE_POSITIONS = 256
FRESH_TOKENS = 2
CONTEXT_SLOTS = 2048
BEAM_TOTAL = 4
BEAM_PAGES = 8


def draw_query(key, part):
    key = jax.random.fold_in(key, 11)
    normal_part = jax.random.normal(key, (BEAM_TOTAL, FRESH_TOKENS, QUERY_HEADS, HEAD_SIZE), jnp.float32)
    return normal_part.reshape(BEAM_TOTAL, FRESH_TOKENS, QUERY_HEADS * HEAD_SIZE).astype(jnp.bfloat16)


def draw_page_table(key, part):
    key = jax.random.fold_in(key, 23)
    scores = jax.random.randint(key, (BEAM_TOTAL, BEAM_PAGES), 0, 1048576, dtype=jnp.int32)
    scores = scores * BEAM_PAGES + jnp.arange(BEAM_PAGES, dtype=jnp.int32)[None, :]
    return jnp.argsort(scores, axis=1, stable=True).astype(jnp.int32)


def set_ends(entries, rng, low, largest):
    dims = entries.shape
    index_at = [jax.random.randint(jax.random.fold_in(rng, axis), (), 0, dims[axis]) for axis in range(len(dims))]
    entries = entries.at[tuple(index_at)].set(low)
    longest = dims.index(max(dims))
    index_at[longest] = (index_at[longest] + 1) % dims[longest]
    return entries.at[tuple(index_at)].set(largest)


def levels(rng, shape, shards, low, top_value):
    gain = 1.0
    for axis_at, blocks in shards:
        heights = jax.random.uniform(jax.random.fold_in(jax.random.fold_in(rng, 6), axis_at), (blocks,), jnp.float32, low / len(shards), top_value / len(shards))
        gain = gain * jnp.repeat(jnp.exp(heights), shape[axis_at] // blocks).reshape((-1,) + (1,) * (len(shape) - 1 - axis_at))
    return gain


def rank_bounds(amount, lean):
    portions = [(1 << 20) // math.isqrt(grade ** lean) + 1 for grade in range(1, amount + 1)]
    scale = 1 + sum(portions) // (1 << 30)
    return np.cumsum(np.array([max(1, weight // scale) for weight in portions]))


def skewed_ids(own_key, shape, amount, lean):
    grid = rank_bounds(amount, lean)
    pick = jax.random.randint(jax.random.fold_in(own_key, 1), shape, 0, int(grid[amount - 1]))
    grade = jnp.searchsorted(jnp.asarray(grid, jnp.int32), pick, side="right")
    return jax.random.permutation(jax.random.fold_in(own_key, 2), amount)[grade].astype(jnp.int32)


def normal_values(stream_key, shape, spread, limit, pieces=(), kind=jnp.bfloat16):
    array = spread * jax.random.normal(stream_key, shape, jnp.float32)
    if pieces:
        array = array * levels(stream_key, shape, pieces, -0.22, 0.18)
    return jnp.clip(array, -limit, limit).astype(kind)


def setup_inputs(seed: int = 0, part: int = 0) -> dict:
    keys = jax.random.split(jax.random.key(seed), 8)
    part_splits = jax.random.split(jax.random.fold_in(keys[7], part), 8)
    return {
        "cache": normal_values(part_splits[0], (BEAM_TOTAL, 2, BEAM_PAGES, PAGE_POSITIONS, KEY_VALUE_HEADS * HEAD_SIZE), 1.0, 6.0, ((0, 4), (2, 2), (4, 2))),
        "query": draw_query(jax.random.fold_in(jax.random.fold_in(keys[7], part), 71), part),
        "fresh_key_values": normal_values(part_splits[2], (BEAM_TOTAL, 2, FRESH_TOKENS, KEY_VALUE_HEADS * HEAD_SIZE), 1.0, 6.0, ((0, 4), (3, 2))),
        "parents": set_ends(skewed_ids(part_splits[3], (BEAM_TOTAL,), BEAM_TOTAL, 2), jax.random.fold_in(part_splits[3], 3), 0, BEAM_TOTAL - 1).astype(jnp.int32),
        "lengths": set_ends(jax.random.randint(part_splits[4], (BEAM_TOTAL,), CONTEXT_SLOTS // 4, CONTEXT_SLOTS + 1), jax.random.fold_in(part_splits[4], 1), CONTEXT_SLOTS // 4, CONTEXT_SLOTS).astype(jnp.int32),
        "page_table": draw_page_table(jax.random.fold_in(jax.random.fold_in(keys[7], part), 71), part),
        "out_weight": normal_values(keys[6], (QUERY_HEADS * HEAD_SIZE, D), (QUERY_HEADS * HEAD_SIZE) ** -0.5, 0.0625, ((0, 2), (1, 8))),
    }


NEG_FILL = -1e+30

def reference(cache, query, fresh_key_values, parents, lengths, page_table, out_weight):
    query_groups = QUERY_HEADS // KEY_VALUE_HEADS
    scale = 1.0 / math.sqrt(HEAD_SIZE)
    page_ids = jnp.arange(BEAM_PAGES, dtype=jnp.int32)
    causal = jnp.arange(FRESH_TOKENS, dtype=jnp.int32)[:, None] >= jnp.arange(FRESH_TOKENS, dtype=jnp.int32)[None, :]

    def one_beam(beam_number):
        parent_id = parents[beam_number]
        stored_cache = lax.dynamic_index_in_dim(cache, parent_id, 0, keepdims=False)
        page_row = lax.dynamic_index_in_dim(page_table, parent_id, 0, keepdims=False)
        length_cap = lengths[parent_id]
        page_num = lax.optimization_barrier(jnp.sum(page_ids[None, :] * (page_row[None, :] == page_ids[:, None]).astype(jnp.int32), axis=1))
        positions = page_num[:, None] * PAGE_POSITIONS + jnp.arange(PAGE_POSITIONS, dtype=jnp.int32)[None, :]
        in_length = (positions < length_cap).reshape(CONTEXT_SLOTS)
        fresh_key_value_pair = lax.dynamic_index_in_dim(fresh_key_values, beam_number, 0, keepdims=False)
        cached_key_rows = jnp.concatenate([stored_cache[0].reshape(CONTEXT_SLOTS, KEY_VALUE_HEADS, HEAD_SIZE), fresh_key_value_pair[0].reshape(FRESH_TOKENS, KEY_VALUE_HEADS, HEAD_SIZE)], axis=0).astype(jnp.float32)
        cached_value_rows = jnp.concatenate([stored_cache[1].reshape(CONTEXT_SLOTS, KEY_VALUE_HEADS, HEAD_SIZE), fresh_key_value_pair[1].reshape(FRESH_TOKENS, KEY_VALUE_HEADS, HEAD_SIZE)], axis=0).astype(jnp.float32)
        allowed = jnp.concatenate([jnp.broadcast_to(in_length[None, :], (FRESH_TOKENS, CONTEXT_SLOTS)), causal], axis=1)
        allowed = allowed[:, None, None, :]
        grouped_queries = lax.dynamic_index_in_dim(query, beam_number, 0, keepdims=False).reshape(FRESH_TOKENS, KEY_VALUE_HEADS, query_groups, HEAD_SIZE).astype(jnp.float32)
        scores = jnp.einsum('tkgd,skd->tkgs', grouped_queries, cached_key_rows, precision=lax.Precision.HIGHEST) * scale
        row_max = lax.optimization_barrier(jnp.max(jnp.where(allowed, scores, NEG_FILL), axis=-1))
        weights = jnp.where(allowed, jnp.exp(scores - row_max[..., None]), 0.0)
        weighted = jnp.einsum('tkgs,skd->tkgd', weights, cached_value_rows, precision=lax.Precision.HIGHEST)
        attended = weighted / lax.optimization_barrier(jnp.sum(weights, axis=-1))[..., None]
        return attended.reshape(FRESH_TOKENS, QUERY_HEADS * HEAD_SIZE).astype(jnp.bfloat16)
    attended_all = lax.map(one_beam, jnp.arange(BEAM_TOTAL, dtype=jnp.int32))
    projected = jnp.dot(attended_all.reshape(BEAM_TOTAL * FRESH_TOKENS, QUERY_HEADS * HEAD_SIZE), out_weight, preferred_element_type=jnp.float32).astype(jnp.bfloat16)
    moved_cache = jnp.take(cache, parents, axis=0)
    return (moved_cache, projected)
```

```python
import math

import jax
import jax.numpy as jnp
from jax import lax
from jax.experimental import pallas as pl
from jax.experimental.pallas import tpu as pltpu
from jax.sharding import PartitionSpec as P

HEAD_SIZE = 128


NEG_FILL = -1e30


def joined(shard, axis, combine):
    everything = jax.tree.map(lambda part: lax.all_gather(part, axis), shard)
    first = jax.tree.map(lambda part: part[0], everything)

    def step(k, so_far):
        return combine(so_far, jax.tree.map(lambda part: part[k], everything))

    return lax.fori_loop(1, lax.axis_size(axis), step, first)


def merge_parts(first, second):
    max_first, total_first, weighted_first = first
    max_second, total_second, weighted_second = second
    max_joint = jnp.maximum(max_first, max_second)
    scale_first = jnp.exp(max_first - max_joint)
    scale_second = jnp.exp(max_second - max_joint)
    return (
        max_joint,
        total_first * scale_first + total_second * scale_second,
        weighted_first * scale_first[..., None] + weighted_second * scale_second[..., None],
    )


def partial_attention(stored_cache, queries, length_caps, page_rows):
    beam_count, _, local_pages, page_len, kv_width = stored_cache.shape
    kv_heads = kv_width // HEAD_SIZE
    new_count = queries.shape[1]
    query_groups = queries.shape[2] // kv_width
    slot_first = lax.axis_index("seq") * local_pages
    slot_ids = slot_first + jnp.arange(local_pages, dtype=jnp.int32)
    page_ids = jnp.arange(page_rows.shape[1], dtype=jnp.int32)
    page_num = jnp.sum(
        page_ids[None, None, :]
        * (page_rows[:, None, :] == slot_ids[None, :, None]).astype(jnp.int32),
        axis=2,
    )
    positions = (
        page_num[:, :, None] * page_len + jnp.arange(page_len, dtype=jnp.int32)[None, None, :]
    )
    in_length = (positions < length_caps[:, None, None]).reshape(beam_count, local_pages * page_len)
    allowed = in_length[:, None, None, None, :]
    cached_key_rows = stored_cache[:, 0].reshape(
        beam_count, local_pages * page_len, kv_heads, HEAD_SIZE
    )
    cached_value_rows = stored_cache[:, 1].reshape(
        beam_count, local_pages * page_len, kv_heads, HEAD_SIZE
    )
    grouped_queries = queries.reshape(beam_count, new_count, kv_heads, query_groups, HEAD_SIZE)
    scores = jnp.einsum(
        "ntkgd,nskd->ntkgs", grouped_queries, cached_key_rows, preferred_element_type=jnp.float32
    ) * (1.0 / math.sqrt(HEAD_SIZE))
    row_max = jnp.max(jnp.where(allowed, scores, NEG_FILL), axis=-1)
    weights = jnp.where(allowed, jnp.exp(scores - row_max[..., None]), 0.0)
    totals = jnp.sum(weights, axis=-1)
    weighted = jnp.einsum(
        "ntkgs,nskd->ntkgd",
        weights,
        cached_value_rows.astype(jnp.float32),
        precision=lax.Precision.HIGHEST,
    )
    return joined((row_max, totals, weighted), "seq", merge_parts)


def finish(merged, queries, new_pairs):
    row_max, totals, weighted = merged
    beam_count, new_count, q_width = queries.shape
    kv_width = new_pairs.shape[-1]
    kv_heads = kv_width // HEAD_SIZE
    query_groups = q_width // kv_width
    grouped_queries = queries.reshape(beam_count, new_count, kv_heads, query_groups, HEAD_SIZE)
    new_keys = new_pairs[:, 0].reshape(beam_count, new_count, kv_heads, HEAD_SIZE)
    new_values = new_pairs[:, 1].reshape(beam_count, new_count, kv_heads, HEAD_SIZE)
    scores = jnp.einsum(
        "ntkgd,nskd->ntkgs", grouped_queries, new_keys, preferred_element_type=jnp.float32
    ) * (1.0 / math.sqrt(HEAD_SIZE))
    causal = (
        jnp.arange(new_count, dtype=jnp.int32)[:, None]
        >= jnp.arange(new_count, dtype=jnp.int32)[None, :]
    )
    allowed = causal[None, :, None, None, :]
    joint_max = jnp.maximum(row_max, jnp.max(jnp.where(allowed, scores, NEG_FILL), axis=-1))
    old_scale = jnp.exp(row_max - joint_max)
    weights = jnp.where(allowed, jnp.exp(scores - joint_max[..., None]), 0.0)
    total_all = totals * old_scale + jnp.sum(weights, axis=-1)
    weighted_all = weighted * old_scale[..., None] + jnp.einsum(
        "ntkgs,nskd->ntkgd",
        weights,
        new_values.astype(jnp.float32),
        precision=lax.Precision.HIGHEST,
    )
    return (
        (weighted_all / total_all[..., None])
        .reshape(beam_count, new_count, q_width)
        .astype(jnp.bfloat16)
    )


def per_device(cache, query, fresh_key_values, parents, lengths, page_table, out_weight):
    beam_dev = cache.shape[0]
    device_here = lax.axis_index("dp")
    own_parents = lax.dynamic_slice_in_dim(parents, device_here * beam_dev, beam_dev)
    own_lengths = jnp.take(lengths, own_parents)
    own_tables = jnp.take(page_table, own_parents, axis=0)
    every_cache = lax.all_gather(cache, "dp", axis=0, tiled=True)
    moved = jnp.take(every_cache, own_parents, axis=0)
    merged = partial_attention(moved, query, own_lengths, own_tables)
    attended = finish(merged, query, fresh_key_values)
    head_rows = attended.reshape(beam_dev * attended.shape[1], attended.shape[2])
    terms = jnp.dot(
        lax.all_gather(head_rows, "dp", axis=0, tiled=True),
        out_weight,
        preferred_element_type=jnp.float32,
    )
    projected = lax.psum_scatter(
        terms.astype(jnp.bfloat16), "tensor", scatter_dimension=0, tiled=True
    )
    return (moved, projected)


MESH = pl.DeviceIdType.MESH
CHUNKS = 16
AHEAD = 6


def chain_kernel(
    parents, lengths, tables, qf, cache, weight,
    moved, spare, second, out,
    own, from_left, from_right, to_right, to_left, moved_buf, spare_buf, held_weight,
    q_all, q_rows, part_send, part_recv, att_all, att_full, out_send, out_recv, need_send, need_recv,
    own_sem, weight_sem, right_send, right_recv, left_send, left_recv, moved_sem, spare_sem,
    q_send_sem, q_recv_sem, att_send_sem, att_recv_sem, pair_send_sem, pair_recv_sem,
):
    me = lax.axis_index("dp")
    core = lax.axis_index("seq")
    tens = lax.axis_index("tensor")
    group = lax.axis_index("groups")
    beams = 4
    kv_heads = qf.shape[0]
    half_heads = kv_heads // 2
    rows = beams * 16
    chunk_rows, kv_width = own.shape[1:]
    page_len = 256
    local_pages = own.shape[0] * chunk_rows // (2 * page_len)
    stored = local_pages * page_len
    mate = {"seq": 1 - core}
    across = {"tensor": 1 - tens}
    other_group = {"groups": 1 - group}

    def far(step):
        return lax.rem(me + step, beams)

    right, left = {"dp": far(1)}, {"dp": far(3)}

    barrier = pltpu.get_barrier_semaphore()
    for peer in [{"dp": far(1)}, {"dp": far(2)}, {"dp": far(3)}, mate, across, other_group]:
        pl.semaphore_signal(barrier, inc=1, device_id=peer, device_id_type=MESH)

    load_own = pltpu.make_async_copy(cache, own, own_sem)
    load_own.start()
    load_weight = pltpu.make_async_copy(weight, held_weight, weight_sem)

    par = [parents[i] for i in range(beams)]
    mine = parents[me]
    low2, low3 = par[2] < 2, par[3] < 2
    high0, high1 = par[0] > 1, par[1] > 1
    twice = (low2 & low3 & (par[2] != par[3])) | (high0 & high1 & (par[0] != par[1]))
    first_right = jnp.where(low3, par[3], par[2])
    first_left = jnp.where(high0, par[0], par[1])
    pass_right = jnp.where(me == 1, first_right == 0, par[3] != 2)
    pass_left = jnp.where(me == 2, first_left == 3, par[0] != 1)
    spare_left = (me == 1) & (par[2] == 0)
    spare_right = (me == 2) & (par[1] == 3)
    take_left, take_right = mine < me, mine > me

    need_send[...] = jnp.full(need_send.shape, jnp.where(twice, 1, 0), jnp.int32)
    q_all[me] = qf[...]
    pl.semaphore_wait(barrier, 6)

    def q_copy(step):
        return pltpu.make_async_remote_copy(
            src_ref=qf, dst_ref=q_all.at[me], send_sem=q_send_sem.at[step],
            recv_sem=q_recv_sem.at[me], device_id={"dp": far(step)}, device_id_type=MESH)

    for step in (1, 2, 3):
        q_copy(step).start()
    need_copy = pltpu.make_async_remote_copy(
        src_ref=need_send, dst_ref=need_recv, send_sem=pair_send_sem.at[3],
        recv_sem=pair_recv_sem.at[3], device_id=other_group, device_id_type=MESH)
    need_copy.start()

    def right_copy(c, source):
        return pltpu.make_async_remote_copy(
            src_ref=source.at[c], dst_ref=from_left.at[c], send_sem=right_send.at[c],
            recv_sem=right_recv.at[c], device_id=right, device_id_type=MESH)

    def left_copy(c, source):
        return pltpu.make_async_remote_copy(
            src_ref=source.at[c], dst_ref=from_right.at[c], send_sem=left_send.at[c],
            recv_sem=left_recv.at[c], device_id=left, device_id_type=MESH)

    middle = (me == 1) | (me == 2)

    def first_send(c):
        @pl.when(me == 0)
        def _():
            right_copy(c, cache).start()

        @pl.when(me == beams - 1)
        def _():
            left_copy(c, cache).start()

    for c in range(AHEAD):
        first_send(c)
    load_own.wait()
    load_weight.start()

    lag_right = jnp.where(me == 1, 0, 1)
    lag_left = jnp.where(me == 2, 0, 1)

    def serve(s, _):
        c_right = s - lag_right
        c_left = s - lag_left

        @pl.when((me > 0) & (c_right >= 0) & (c_right < CHUNKS))
        def _():
            right_copy(c_right, to_right).wait_recv()

            @pl.when(middle)
            def _():
                to_right[c_right] = jnp.where(pass_right, from_left[c_right], own[c_right])
                right_copy(c_right, to_right).start()

        @pl.when((me < beams - 1) & (c_left >= 0) & (c_left < CHUNKS))
        def _():
            left_copy(c_left, to_left).wait_recv()

            @pl.when(middle)
            def _():
                to_left[c_left] = jnp.where(pass_left, from_right[c_left], own[c_left])
                left_copy(c_left, to_left).start()

        @pl.when(s + AHEAD < CHUNKS)
        def _():
            first_send(s + AHEAD)

        @pl.when(s >= 1)
        def _():
            c = s - 1
            moved_buf[c] = jnp.where(
                take_left, from_left[c], jnp.where(take_right, from_right[c], own[c]))
            pltpu.make_async_copy(moved_buf.at[c], moved.at[c], moved_sem.at[c]).start()

            @pl.when(middle)
            def _():
                spare_buf[c] = jnp.where(
                    spare_left, from_left[c], jnp.where(spare_right, from_right[c], own[c]))
                pltpu.make_async_copy(spare_buf.at[c], spare.at[c], spare_sem.at[c]).start()

        return 0

    def serves(lo, hi):
        lax.fori_loop(lo, hi, serve, 0)

    row_ids = lax.broadcasted_iota(jnp.int32, (rows, 1), 0)
    row_beam = lax.rem(row_ids, 2 * beams) // 2
    row_token = lax.rem(row_ids, 2)
    row_parent = jnp.zeros((rows, 1), jnp.int32)
    for i in range(beams):
        row_parent = jnp.where(row_beam == i, par[i], row_parent)
    slot_ids = lax.broadcasted_iota(jnp.int32, (1, stored), 1)
    page_base = jnp.zeros((1, stored), jnp.int32)
    for slot in range(local_pages):
        page = jnp.int32(0)
        for j in range(tables.shape[1]):
            page = page + jnp.where(tables[me, j] == core * local_pages + slot, j, 0)
        page_base = jnp.where(slot_ids // page_len == slot, page * page_len, page_base)
    allowed = page_base + lax.rem(slot_ids, page_len) < lengths[me]
    scale = 1.0 / math.sqrt(HEAD_SIZE)

    def queries_ready():
        for step in (1, 2, 3):
            pltpu.make_async_remote_copy(
                src_ref=qf, dst_ref=q_all.at[far(step)], send_sem=q_send_sem.at[step],
                recv_sem=q_recv_sem.at[far(step)], device_id={"dp": far(step)},
                device_id_type=MESH).wait_recv()
        r = lax.broadcasted_iota(jnp.int32, (rows, rows), 0)
        col = lax.broadcasted_iota(jnp.int32, (rows, rows), 1)
        place = lax.rem(r, 2 * beams) // 2 * 16 + r // (2 * beams) * 2 + lax.rem(r, 2)
        order = jnp.where(place == col, 1.0, 0.0).astype(jnp.bfloat16)
        for k in range(kv_heads):
            stacked = jnp.concatenate([q_all[i, k, 0:16, :] for i in range(beams)], axis=0)
            q_rows[k] = jnp.dot(order, stacked, preferred_element_type=jnp.float32).astype(
                jnp.bfloat16)

    half = own.shape[0] // 2

    def head(k, store, at):
        lanes = pl.ds(pl.multiple_of(k * HEAD_SIZE, HEAD_SIZE), HEAD_SIZE)
        keys = own[0:half, :, lanes].reshape(stored, HEAD_SIZE)
        values = own[half:2 * half, :, lanes].reshape(stored, HEAD_SIZE)
        scores = lax.dot_general(
            q_rows[k], keys, (((1,), (1,)), ((), ())), preferred_element_type=jnp.float32) * scale
        top = jnp.max(jnp.where(allowed, scores, NEG_FILL), axis=1, keepdims=True)
        weights = jnp.where(allowed, jnp.exp(scores - top), 0.0)
        total = jnp.sum(weights, axis=1, keepdims=True)
        coarse = weights.astype(jnp.bfloat16)
        fine = (weights - coarse.astype(jnp.float32)).astype(jnp.bfloat16)
        both = jnp.dot(
            jnp.concatenate([coarse, fine], axis=0), values, preferred_element_type=jnp.float32)
        store[at, 0] = both[:rows] + both[rows:]
        lane = lax.broadcasted_iota(jnp.int32, (rows, HEAD_SIZE), 1)
        store[at, 1] = jnp.where(lane < 1, top, total)

    part_copy = pltpu.make_async_remote_copy(
        src_ref=part_send.at[0], dst_ref=part_recv, send_sem=pair_send_sem.at[0],
        recv_sem=pair_recv_sem.at[0], device_id=mate, device_id_type=MESH)

    def spread(k, first_row):
        full = jnp.zeros((rows, HEAD_SIZE), jnp.float32)
        for i in range(beams):
            block = q_all[i, k, 16:32, :].astype(jnp.float32)[first_row:first_row + 1]
            full = jnp.where(row_beam == i, block, full)
        return full

    def att_copy(step):
        return pltpu.make_async_remote_copy(
            src_ref=att_all.at[me], dst_ref=att_all.at[me], send_sem=att_send_sem.at[step],
            recv_sem=att_recv_sem.at[me], device_id={"dp": far(step)}, device_id_type=MESH)

    def merge():
        part_copy.wait_recv()
        for at in range(half_heads):
            k = core * half_heads + at
            stat_here, stat_there = part_send[1, at, 1], part_recv[at, 1]
            top_here, top_there = stat_here[:, 0:1], stat_there[:, 0:1]
            q_here = q_rows[k].astype(jnp.float32)
            score0 = jnp.sum(q_here * spread(k, 0), axis=1, keepdims=True) * scale
            score1 = jnp.sum(q_here * spread(k, 1), axis=1, keepdims=True) * scale
            score1 = jnp.where(row_token == 1, score1, NEG_FILL)
            top = jnp.maximum(jnp.maximum(top_here, top_there), jnp.maximum(score0, score1))
            scale_here, scale_there = jnp.exp(top_here - top), jnp.exp(top_there - top)
            weight0 = jnp.exp(score0 - top)
            weight1 = jnp.where(row_token == 1, jnp.exp(score1 - top), 0.0)
            total = (stat_here[:, 1:2] * scale_here + stat_there[:, 1:2] * scale_there
                     + weight0 + weight1)
            weighted = (part_send[1, at, 0] * scale_here + part_recv[at, 0] * scale_there
                        + weight0 * spread(k, 2) + weight1 * spread(k, 3))
            att_all[me, at] = (weighted / total).astype(jnp.bfloat16)
        for step in (1, 2, 3):
            att_copy(step).start()

    mate_copy = pltpu.make_async_remote_copy(
        src_ref=att_full.at[core], dst_ref=att_full.at[core], send_sem=pair_send_sem.at[1],
        recv_sem=pair_recv_sem.at[1], device_id=mate, device_id_type=MESH)
    mate_wait = pltpu.make_async_remote_copy(
        src_ref=att_full.at[1 - core], dst_ref=att_full.at[1 - core],
        send_sem=pair_send_sem.at[1],
        recv_sem=pair_recv_sem.at[1], device_id=mate, device_id_type=MESH)

    def pick():
        for step in (1, 2, 3):
            pltpu.make_async_remote_copy(
                src_ref=att_all.at[me], dst_ref=att_all.at[far(step)],
                send_sem=att_send_sem.at[step], recv_sem=att_recv_sem.at[far(step)],
                device_id={"dp": far(step)}, device_id_type=MESH).wait_recv()
        for at in range(half_heads):
            chosen = jnp.zeros((rows, HEAD_SIZE), jnp.float32)
            for i in range(beams):
                chosen = jnp.where(row_parent == i, att_all[i, at].astype(jnp.float32), chosen)
            att_full[core, at] = chosen.astype(jnp.bfloat16)
        mate_copy.start()

    out_copy = pltpu.make_async_remote_copy(
        src_ref=out_send.at[1 - tens], dst_ref=out_recv, send_sem=pair_send_sem.at[2],
        recv_sem=pair_recv_sem.at[2], device_id=across, device_id_type=MESH)
    row_count = 2 * beams

    def project():
        mate_wait.wait_recv()
        load_weight.wait()
        pieces = []
        for k in range(kv_heads):
            whole = att_full[k // half_heads, k % half_heads].astype(jnp.float32)
            pieces += [whole[g * row_count:(g + 1) * row_count] for g in range(rows // row_count)]
        flat = jnp.concatenate(pieces, axis=1).astype(jnp.bfloat16)
        tile = 256

        def column(j, _):
            lanes = pl.ds(pl.multiple_of(j * tile, tile), tile)
            term = jnp.dot(flat, held_weight[:, lanes], preferred_element_type=jnp.float32)
            share = row_count // 2
            out_send[0, :, lanes] = term[:share]
            out_send[1, :, lanes] = term[share:]
            return 0

        lax.fori_loop(0, held_weight.shape[1] // tile, column, 0)
        out_copy.start()

    queries_ready()
    head((1 - core) * half_heads, part_send.at[0], 0)
    serves(0, 1)
    head((1 - core) * half_heads + 1, part_send.at[0], 1)
    part_copy.start()
    serves(1, 2)
    head(core * half_heads, part_send.at[1], 0)
    serves(2, 3)
    head(core * half_heads + 1, part_send.at[1], 1)
    serves(3, 4)
    merge()
    serves(4, 9)
    pick()
    serves(9, 11)
    project()
    serves(11, CHUNKS + 1)
    out_copy.wait_recv()
    out[...] = (out_send[tens] + out_recv[...]).astype(jnp.bfloat16)
    need_copy.wait_recv()
    second[...] = jnp.maximum(need_send[...], need_recv[...])

    def drain(c, _):
        pltpu.make_async_copy(moved_buf.at[c], moved.at[c], moved_sem.at[c]).wait()

        @pl.when(middle)
        def _():
            pltpu.make_async_copy(spare_buf.at[c], spare.at[c], spare_sem.at[c]).wait()

        @pl.when(me < beams - 1)
        def _():
            right_copy(c, to_right).wait_send()

        @pl.when(me > 0)
        def _():
            left_copy(c, to_left).wait_send()

        return 0

    lax.fori_loop(0, CHUNKS, drain, 0)
    for step in (1, 2, 3):
        q_copy(step).wait_send()
        att_copy(step).wait_send()
    part_copy.wait_send()
    mate_copy.wait_send()
    out_copy.wait_send()
    need_copy.wait_send()


def four_beams(cache, query, fresh_key_values, parents, lengths, page_table, out_weight):
    _, halves, pages, page_len, kv_width = cache.shape
    kv_heads = kv_width // HEAD_SIZE
    groups = query.shape[2] // kv_width
    chunk_shape = (CHUNKS, halves * pages * page_len // CHUNKS, kv_width)
    q_part = query.reshape(2, kv_heads, groups, HEAD_SIZE).transpose(1, 2, 0, 3)
    q_part = q_part.reshape(kv_heads, groups * 2, HEAD_SIZE)
    fresh_part = fresh_key_values.reshape(4, kv_heads, HEAD_SIZE).transpose(1, 0, 2)
    qf = jnp.concatenate(
        [q_part, jnp.pad(fresh_part, ((0, 0), (0, 12), (0, 0)))], axis=1)
    rows = 4 * 16
    out_rows, out_columns = 4, out_weight.shape[1]
    vmem = pltpu.VMEM
    half_heads = kv_heads // 2
    big = vmem(chunk_shape, jnp.bfloat16)
    dma = pltpu.SemaphoreType.DMA
    smem_spec = pl.BlockSpec(memory_space=pltpu.SMEM)
    vmem_spec = pl.BlockSpec(memory_space=pltpu.VMEM)
    any_spec = pl.BlockSpec(memory_space=pl.ANY)
    moved, spare, second, out = pl.pallas_call(
        chain_kernel,
        out_shape=[
            jax.ShapeDtypeStruct(chunk_shape, jnp.bfloat16),
            jax.ShapeDtypeStruct(chunk_shape, jnp.bfloat16),
            jax.ShapeDtypeStruct((8, 128), jnp.int32),
            jax.ShapeDtypeStruct((out_rows, out_columns), jnp.bfloat16),
        ],
        in_specs=[smem_spec, smem_spec, smem_spec, vmem_spec, any_spec, any_spec],
        out_specs=[any_spec, any_spec, vmem_spec, vmem_spec],
        scratch_shapes=[
            big, big, big, big, big, big, big,
            vmem(out_weight.shape, jnp.bfloat16),
            vmem((4, kv_heads, 32, HEAD_SIZE), jnp.bfloat16),
            vmem((kv_heads, rows, HEAD_SIZE), jnp.bfloat16),
            vmem((2, half_heads, 2, rows, HEAD_SIZE), jnp.float32),
            vmem((half_heads, 2, rows, HEAD_SIZE), jnp.float32),
            vmem((4, half_heads, rows, HEAD_SIZE), jnp.bfloat16),
            vmem((2, half_heads, rows, HEAD_SIZE), jnp.bfloat16),
            vmem((2, out_rows, out_columns), jnp.float32),
            vmem((out_rows, out_columns), jnp.float32),
            vmem((8, 128), jnp.int32),
            vmem((8, 128), jnp.int32),
            dma, dma,
            dma((CHUNKS,)), dma((CHUNKS,)), dma((CHUNKS,)), dma((CHUNKS,)),
            dma((CHUNKS,)), dma((CHUNKS,)),
            dma((4,)), dma((4,)), dma((4,)), dma((4,)), dma((4,)), dma((4,)),
        ],
        compiler_params=pltpu.CompilerParams(
            collective_id=0, has_side_effects=True, vmem_limit_bytes=48 * 1024 * 1024),
        name="chain",
    )(parents, lengths, page_table, qf, cache.reshape(chunk_shape), out_weight)

    here = lax.axis_index("dp")
    low = (parents[2] < 2) & (parents[3] < 2) & (parents[2] != parents[3]) & (here == 2)
    high = (parents[0] > 1) & (parents[1] > 1) & (parents[0] != parents[1]) & (here == 1)

    def again(first, payload):
        arrived = lax.ppermute(payload, "dp", [(1, 2), (2, 1)])
        return jnp.where(low | high, arrived, first)

    moved = lax.cond(second[0, 0] > 0, again, lambda first, payload: first, moved, spare)
    return (moved.reshape(cache.shape), out)


def solution(mesh):
    in_specs = (
        P(("groups", "dp"), None, "seq", None, "tensor"),
        P(("groups", "dp"), None, "tensor"),
        P(("groups", "dp"), None, None, "tensor"),
        P("groups"),
        P("groups"),
        P("groups", None),
        P("tensor", ("dp", "seq")),
    )
    out_specs = (
        P(("groups", "dp"), None, "seq", None, "tensor"),
        P(("groups", "tensor"), ("dp", "seq")),
    )
    sizes = tuple(mesh.shape[axis] for axis in ("groups", "dp", "tensor", "seq"))
    body = four_beams if sizes == (2, 4, 2, 2) else per_device
    return jax.shard_map(
        body, mesh=mesh, in_specs=in_specs, out_specs=out_specs, check_vma=False
    )
```

```python
import math

import jax
import jax.numpy as jnp
from jax import lax
from jax.experimental import pallas as pl
from jax.experimental.pallas import tpu as pltpu
from jax.sharding import PartitionSpec as P

HEAD_SIZE = 128


NEG_FILL = -1e30


def joined(shard, axis, combine):
    everything = jax.tree.map(lambda part: lax.all_gather(part, axis), shard)
    first = jax.tree.map(lambda part: part[0], everything)

    def step(k, so_far):
        return combine(so_far, jax.tree.map(lambda part: part[k], everything))

    return lax.fori_loop(1, lax.axis_size(axis), step, first)


def merge_parts(first, second):
    max_first, total_first, weighted_first = first
    max_second, total_second, weighted_second = second
    max_joint = jnp.maximum(max_first, max_second)
    scale_first = jnp.exp(max_first - max_joint)
    scale_second = jnp.exp(max_second - max_joint)
    return (
        max_joint,
        total_first * scale_first + total_second * scale_second,
        weighted_first * scale_first[..., None] + weighted_second * scale_second[..., None],
    )


def partial_attention(stored_cache, queries, length_caps, page_rows):
    beam_count, _, local_pages, page_len, kv_width = stored_cache.shape
    kv_heads = kv_width // HEAD_SIZE
    new_count = queries.shape[1]
    query_groups = queries.shape[2] // kv_width
    slot_first = lax.axis_index("seq") * local_pages
    slot_ids = slot_first + jnp.arange(local_pages, dtype=jnp.int32)
    page_ids = jnp.arange(page_rows.shape[1], dtype=jnp.int32)
    page_num = jnp.sum(
        page_ids[None, None, :]
        * (page_rows[:, None, :] == slot_ids[None, :, None]).astype(jnp.int32),
        axis=2,
    )
    positions = (
        page_num[:, :, None] * page_len + jnp.arange(page_len, dtype=jnp.int32)[None, None, :]
    )
    in_length = (positions < length_caps[:, None, None]).reshape(beam_count, local_pages * page_len)
    allowed = in_length[:, None, None, None, :]
    cached_key_rows = stored_cache[:, 0].reshape(
        beam_count, local_pages * page_len, kv_heads, HEAD_SIZE
    )
    cached_value_rows = stored_cache[:, 1].reshape(
        beam_count, local_pages * page_len, kv_heads, HEAD_SIZE
    )
    grouped_queries = queries.reshape(beam_count, new_count, kv_heads, query_groups, HEAD_SIZE)
    scores = jnp.einsum(
        "ntkgd,nskd->ntkgs", grouped_queries, cached_key_rows, preferred_element_type=jnp.float32
    ) * (1.0 / math.sqrt(HEAD_SIZE))
    row_max = jnp.max(jnp.where(allowed, scores, NEG_FILL), axis=-1)
    weights = jnp.where(allowed, jnp.exp(scores - row_max[..., None]), 0.0)
    totals = jnp.sum(weights, axis=-1)
    weighted = jnp.einsum(
        "ntkgs,nskd->ntkgd",
        weights,
        cached_value_rows.astype(jnp.float32),
        precision=lax.Precision.HIGHEST,
    )
    return joined((row_max, totals, weighted), "seq", merge_parts)


def finish(merged, queries, new_pairs):
    row_max, totals, weighted = merged
    beam_count, new_count, q_width = queries.shape
    kv_width = new_pairs.shape[-1]
    kv_heads = kv_width // HEAD_SIZE
    query_groups = q_width // kv_width
    grouped_queries = queries.reshape(beam_count, new_count, kv_heads, query_groups, HEAD_SIZE)
    new_keys = new_pairs[:, 0].reshape(beam_count, new_count, kv_heads, HEAD_SIZE)
    new_values = new_pairs[:, 1].reshape(beam_count, new_count, kv_heads, HEAD_SIZE)
    scores = jnp.einsum(
        "ntkgd,nskd->ntkgs", grouped_queries, new_keys, preferred_element_type=jnp.float32
    ) * (1.0 / math.sqrt(HEAD_SIZE))
    causal = (
        jnp.arange(new_count, dtype=jnp.int32)[:, None]
        >= jnp.arange(new_count, dtype=jnp.int32)[None, :]
    )
    allowed = causal[None, :, None, None, :]
    joint_max = jnp.maximum(row_max, jnp.max(jnp.where(allowed, scores, NEG_FILL), axis=-1))
    old_scale = jnp.exp(row_max - joint_max)
    weights = jnp.where(allowed, jnp.exp(scores - joint_max[..., None]), 0.0)
    total_all = totals * old_scale + jnp.sum(weights, axis=-1)
    weighted_all = weighted * old_scale[..., None] + jnp.einsum(
        "ntkgs,nskd->ntkgd",
        weights,
        new_values.astype(jnp.float32),
        precision=lax.Precision.HIGHEST,
    )
    return (
        (weighted_all / total_all[..., None])
        .reshape(beam_count, new_count, q_width)
        .astype(jnp.bfloat16)
    )


def per_device(cache, query, fresh_key_values, parents, lengths, page_table, out_weight):
    beam_dev = cache.shape[0]
    device_here = lax.axis_index("dp")
    own_parents = lax.dynamic_slice_in_dim(parents, device_here * beam_dev, beam_dev)
    own_lengths = jnp.take(lengths, own_parents)
    own_tables = jnp.take(page_table, own_parents, axis=0)
    every_cache = lax.all_gather(cache, "dp", axis=0, tiled=True)
    moved = jnp.take(every_cache, own_parents, axis=0)
    merged = partial_attention(moved, query, own_lengths, own_tables)
    attended = finish(merged, query, fresh_key_values)
    head_rows = attended.reshape(beam_dev * attended.shape[1], attended.shape[2])
    terms = jnp.dot(
        lax.all_gather(head_rows, "dp", axis=0, tiled=True),
        out_weight,
        preferred_element_type=jnp.float32,
    )
    projected = lax.psum_scatter(
        terms.astype(jnp.bfloat16), "tensor", scatter_dimension=0, tiled=True
    )
    return (moved, projected)


MESH = pl.DeviceIdType.MESH
CHUNKS = 32
AHEAD = 4
END_LAG = 7
MID_LAG = 2


def chain_kernel(
    parents_in, lengths_in, tables_in, qf, cache, weight,
    moved, spare, second, out,
    parents, lengths, tables, own, from_left, from_right, to_right, to_left, moved_buf, spare_buf, held_weight,
    q_all, q_rows, part_send, part_recv, att_all, att_full, out_send, out_recv, need_send, need_recv,
    small_sem, own_sem, weight_sem, right_send, right_recv, left_send, left_recv, moved_sem, spare_sem,
    q_send_sem, q_recv_sem, att_send_sem, att_recv_sem, pair_send_sem, pair_recv_sem,
):
    me = lax.axis_index("dp")
    core = lax.axis_index("seq")
    tens = lax.axis_index("tensor")
    group = lax.axis_index("groups")
    beams = 4
    kv_heads = qf.shape[0]
    half_heads = kv_heads // 2
    rows = beams * 16
    chunk_rows, kv_width = own.shape[1:]
    page_len = 256
    local_pages = own.shape[0] * chunk_rows // (2 * page_len)
    stored = local_pages * page_len
    mate = {"seq": 1 - core}
    across = {"tensor": 1 - tens}
    other_group = {"groups": 1 - group}

    def far(step):
        return lax.rem(me + step, beams)

    right, left = {"dp": far(1)}, {"dp": far(3)}

    barrier = pltpu.get_barrier_semaphore()
    for peer in [{"dp": far(1)}, {"dp": far(2)}, {"dp": far(3)}, mate, across, other_group]:
        pl.semaphore_signal(barrier, inc=1, device_id=peer, device_id_type=MESH)

    smalls = [
        pltpu.make_async_copy(source, target, small_sem.at[i])
        for i, (source, target) in enumerate(
            [(parents_in, parents), (lengths_in, lengths), (tables_in, tables)])
    ]
    for small in smalls:
        small.start()
    load_own = pltpu.make_async_copy(cache, own, own_sem)
    load_own.start()
    load_weight = pltpu.make_async_copy(weight, held_weight, weight_sem)

    q_all[me] = qf[...]
    pl.semaphore_wait(barrier, 6)

    def q_copy(step):
        return pltpu.make_async_remote_copy(
            src_ref=qf, dst_ref=q_all.at[me], send_sem=q_send_sem.at[step],
            recv_sem=q_recv_sem.at[me], device_id={"dp": far(step)}, device_id_type=MESH)

    for step in (1, 2, 3):
        q_copy(step).start()
    def right_copy(c, source):
        return pltpu.make_async_remote_copy(
            src_ref=source.at[c], dst_ref=from_left.at[c], send_sem=right_send.at[c],
            recv_sem=right_recv.at[c], device_id=right, device_id_type=MESH)

    def left_copy(c, source):
        return pltpu.make_async_remote_copy(
            src_ref=source.at[c], dst_ref=from_right.at[c], send_sem=left_send.at[c],
            recv_sem=left_recv.at[c], device_id=left, device_id_type=MESH)

    middle = (me == 1) | (me == 2)

    def first_send(c):
        @pl.when(me == 0)
        def _():
            right_copy(c, cache).start()

        @pl.when(me == beams - 1)
        def _():
            left_copy(c, cache).start()

    for c in range(AHEAD):
        first_send(c)
    for small in smalls:
        small.wait()
    par = [parents[i] for i in range(beams)]
    mine = parents[me]
    low2, low3 = par[2] < 2, par[3] < 2
    high0, high1 = par[0] > 1, par[1] > 1
    twice = (low2 & low3 & (par[2] != par[3])) | (high0 & high1 & (par[0] != par[1]))
    first_right = jnp.where(low3, par[3], par[2])
    first_left = jnp.where(high0, par[0], par[1])
    pass_right = jnp.where(me == 1, first_right == 0, par[3] != 2)
    pass_left = jnp.where(me == 2, first_left == 3, par[0] != 1)
    spare_left = (me == 1) & (par[2] == 0)
    spare_right = (me == 2) & (par[1] == 3)
    take_left, take_right = mine < me, mine > me

    need_send[...] = jnp.full(need_send.shape, jnp.where(twice, 1, 0), jnp.int32)
    need_copy = pltpu.make_async_remote_copy(
        src_ref=need_send, dst_ref=need_recv, send_sem=pair_send_sem.at[3],
        recv_sem=pair_recv_sem.at[3], device_id=other_group, device_id_type=MESH)
    need_copy.start()

    load_own.wait()
    load_weight.start()

    ends = (me == 0) | (me == beams - 1)
    lag_right = jnp.where(me == 1, 0, jnp.where(me == 2, MID_LAG, END_LAG))
    lag_left = jnp.where(me == 2, 0, jnp.where(me == 1, MID_LAG, END_LAG))
    lag_moved = jnp.where(ends, END_LAG, MID_LAG)

    def serve(s, _):
        @pl.when(s < CHUNKS - AHEAD)
        def _():
            @pl.when(me == 0)
            def _():
                right_copy(s, cache).wait_send()

            @pl.when(me == beams - 1)
            def _():
                left_copy(s, cache).wait_send()

            first_send(s + AHEAD)

        c_right = s - lag_right
        c_left = s - lag_left

        @pl.when((me > 0) & (c_right >= 0) & (c_right < CHUNKS))
        def _():
            right_copy(c_right, to_right).wait_recv()

            @pl.when(middle)
            def _():
                to_right[c_right] = jnp.where(pass_right, from_left[c_right], own[c_right])
                right_copy(c_right, to_right).start()

        @pl.when((me < beams - 1) & (c_left >= 0) & (c_left < CHUNKS))
        def _():
            left_copy(c_left, to_left).wait_recv()

            @pl.when(middle)
            def _():
                to_left[c_left] = jnp.where(pass_left, from_right[c_left], own[c_left])
                left_copy(c_left, to_left).start()

        c = s - lag_moved

        @pl.when((c >= 0) & (c < CHUNKS))
        def _():
            moved_buf[c] = jnp.where(
                take_left, from_left[c], jnp.where(take_right, from_right[c], own[c]))
            pltpu.make_async_copy(moved_buf.at[c], moved.at[c], moved_sem.at[c]).start()

            @pl.when(middle)
            def _():
                spare_buf[c] = jnp.where(
                    spare_left, from_left[c], jnp.where(spare_right, from_right[c], own[c]))
                pltpu.make_async_copy(spare_buf.at[c], spare.at[c], spare_sem.at[c]).start()

        return 0

    def serves(lo, hi):
        lax.fori_loop(lo, hi, serve, 0)

    row_ids = lax.broadcasted_iota(jnp.int32, (rows, 1), 0)
    row_beam = lax.rem(row_ids, 2 * beams) // 2
    row_token = lax.rem(row_ids, 2)
    row_parent = jnp.zeros((rows, 1), jnp.int32)
    for i in range(beams):
        row_parent = jnp.where(row_beam == i, par[i], row_parent)
    slot_ids = lax.broadcasted_iota(jnp.int32, (1, stored), 1)
    page_base = jnp.zeros((1, stored), jnp.int32)
    for slot in range(local_pages):
        page = jnp.int32(0)
        for j in range(tables.shape[1]):
            page = page + jnp.where(tables[me, j] == core * local_pages + slot, j, 0)
        page_base = jnp.where(slot_ids // page_len == slot, page * page_len, page_base)
    allowed = page_base + lax.rem(slot_ids, page_len) < lengths[me]
    scale = 1.0 / math.sqrt(HEAD_SIZE)

    def queries_ready():
        for step in (1, 2, 3):
            pltpu.make_async_remote_copy(
                src_ref=qf, dst_ref=q_all.at[far(step)], send_sem=q_send_sem.at[step],
                recv_sem=q_recv_sem.at[far(step)], device_id={"dp": far(step)},
                device_id_type=MESH).wait_recv()
        r = lax.broadcasted_iota(jnp.int32, (rows, rows), 0)
        col = lax.broadcasted_iota(jnp.int32, (rows, rows), 1)
        place = lax.rem(r, 2 * beams) // 2 * 16 + r // (2 * beams) * 2 + lax.rem(r, 2)
        order = jnp.where(place == col, 1.0, 0.0).astype(jnp.bfloat16)
        for k in range(kv_heads):
            stacked = jnp.concatenate([q_all[i, k, 0:16, :] for i in range(beams)], axis=0)
            q_rows[k] = jnp.dot(order, stacked, preferred_element_type=jnp.float32).astype(
                jnp.bfloat16)

    half = own.shape[0] // 2

    def head(k, store, at):
        lanes = pl.ds(pl.multiple_of(k * HEAD_SIZE, HEAD_SIZE), HEAD_SIZE)
        keys = own[0:half, :, lanes].reshape(stored, HEAD_SIZE)
        values = own[half:2 * half, :, lanes].reshape(stored, HEAD_SIZE)
        scores = lax.dot_general(
            q_rows[k], keys, (((1,), (1,)), ((), ())), preferred_element_type=jnp.float32) * scale
        top = jnp.max(jnp.where(allowed, scores, NEG_FILL), axis=1, keepdims=True)
        weights = jnp.where(allowed, jnp.exp(scores - top), 0.0)
        total = jnp.sum(weights, axis=1, keepdims=True)
        coarse = weights.astype(jnp.bfloat16)
        fine = (weights - coarse.astype(jnp.float32)).astype(jnp.bfloat16)
        both = jnp.dot(
            jnp.concatenate([coarse, fine], axis=0), values, preferred_element_type=jnp.float32)
        store[at, 0] = both[:rows] + both[rows:]
        lane = lax.broadcasted_iota(jnp.int32, (rows, HEAD_SIZE), 1)
        store[at, 1] = jnp.where(lane < 1, top, total)

    part_copy = pltpu.make_async_remote_copy(
        src_ref=part_send.at[0], dst_ref=part_recv, send_sem=pair_send_sem.at[0],
        recv_sem=pair_recv_sem.at[0], device_id=mate, device_id_type=MESH)

    def spread(k, first_row):
        full = jnp.zeros((rows, HEAD_SIZE), jnp.float32)
        for i in range(beams):
            block = q_all[i, k, 16:32, :].astype(jnp.float32)[first_row:first_row + 1]
            full = jnp.where(row_beam == i, block, full)
        return full

    def att_copy(step):
        return pltpu.make_async_remote_copy(
            src_ref=att_all.at[me], dst_ref=att_all.at[me], send_sem=att_send_sem.at[step],
            recv_sem=att_recv_sem.at[me], device_id={"dp": far(step)}, device_id_type=MESH)

    def merge():
        part_copy.wait_recv()
        for at in range(half_heads):
            k = core * half_heads + at
            stat_here, stat_there = part_send[1, at, 1], part_recv[at, 1]
            top_here, top_there = stat_here[:, 0:1], stat_there[:, 0:1]
            q_here = q_rows[k].astype(jnp.float32)
            score0 = jnp.sum(q_here * spread(k, 0), axis=1, keepdims=True) * scale
            score1 = jnp.sum(q_here * spread(k, 1), axis=1, keepdims=True) * scale
            score1 = jnp.where(row_token == 1, score1, NEG_FILL)
            top = jnp.maximum(jnp.maximum(top_here, top_there), jnp.maximum(score0, score1))
            scale_here, scale_there = jnp.exp(top_here - top), jnp.exp(top_there - top)
            weight0 = jnp.exp(score0 - top)
            weight1 = jnp.where(row_token == 1, jnp.exp(score1 - top), 0.0)
            total = (stat_here[:, 1:2] * scale_here + stat_there[:, 1:2] * scale_there
                     + weight0 + weight1)
            weighted = (part_send[1, at, 0] * scale_here + part_recv[at, 0] * scale_there
                        + weight0 * spread(k, 2) + weight1 * spread(k, 3))
            att_all[me, at] = (weighted / total).astype(jnp.bfloat16)
        for step in (1, 2, 3):
            att_copy(step).start()

    mate_copy = pltpu.make_async_remote_copy(
        src_ref=att_full.at[core], dst_ref=att_full.at[core], send_sem=pair_send_sem.at[1],
        recv_sem=pair_recv_sem.at[1], device_id=mate, device_id_type=MESH)
    mate_wait = pltpu.make_async_remote_copy(
        src_ref=att_full.at[1 - core], dst_ref=att_full.at[1 - core],
        send_sem=pair_send_sem.at[1],
        recv_sem=pair_recv_sem.at[1], device_id=mate, device_id_type=MESH)

    def pick():
        for step in (1, 2, 3):
            pltpu.make_async_remote_copy(
                src_ref=att_all.at[me], dst_ref=att_all.at[far(step)],
                send_sem=att_send_sem.at[step], recv_sem=att_recv_sem.at[far(step)],
                device_id={"dp": far(step)}, device_id_type=MESH).wait_recv()
        for at in range(half_heads):
            chosen = jnp.zeros((rows, HEAD_SIZE), jnp.float32)
            for i in range(beams):
                chosen = jnp.where(row_parent == i, att_all[i, at].astype(jnp.float32), chosen)
            att_full[core, at] = chosen.astype(jnp.bfloat16)
        mate_copy.start()

    out_copy = pltpu.make_async_remote_copy(
        src_ref=out_send.at[1 - tens], dst_ref=out_recv, send_sem=pair_send_sem.at[2],
        recv_sem=pair_recv_sem.at[2], device_id=across, device_id_type=MESH)
    row_count = 2 * beams

    tile = 256
    column_tiles = held_weight.shape[1] // tile

    def flatten():
        mate_wait.wait_recv()
        load_weight.wait()
        pieces = []
        for k in range(kv_heads):
            whole = att_full[k // half_heads, k % half_heads].astype(jnp.float32)
            pieces += [whole[g * row_count:(g + 1) * row_count] for g in range(rows // row_count)]
        return jnp.concatenate(pieces, axis=1).astype(jnp.bfloat16)

    def column(flat, j):
        lanes = pl.ds(pl.multiple_of(j * tile, tile), tile)
        term = jnp.dot(flat, held_weight[:, lanes], preferred_element_type=jnp.float32)
        share = row_count // 2
        out_send[0, :, lanes] = term[:share]
        out_send[1, :, lanes] = term[share:]
        return serve(24 + j, 0)

    queries_ready()
    serves(0, 1)
    head((1 - core) * half_heads, part_send.at[0], 0)
    serves(1, 2)
    head((1 - core) * half_heads + 1, part_send.at[0], 1)
    part_copy.start()
    serves(2, 4)
    head(core * half_heads, part_send.at[1], 0)
    serves(4, 6)
    head(core * half_heads + 1, part_send.at[1], 1)
    serves(6, 8)
    merge()
    serves(8, 20)
    pick()
    serves(20, 24)
    flat = flatten()
    lax.fori_loop(0, column_tiles, lambda j, _: column(flat, j), 0)
    out_copy.start()
    serves(24 + column_tiles, CHUNKS + END_LAG)
    out_copy.wait_recv()
    out[...] = (out_send[tens] + out_recv[...]).astype(jnp.bfloat16)
    need_copy.wait_recv()
    second[...] = jnp.maximum(need_send[...], need_recv[...])

    def drain(c, _):
        pltpu.make_async_copy(moved_buf.at[c], moved.at[c], moved_sem.at[c]).wait()

        @pl.when(middle)
        def _():
            pltpu.make_async_copy(spare_buf.at[c], spare.at[c], spare_sem.at[c]).wait()

        late = (c >= CHUNKS - AHEAD)

        @pl.when(middle | ((me == 0) & late))
        def _():
            right_copy(c, to_right).wait_send()

        @pl.when(middle | ((me == beams - 1) & late))
        def _():
            left_copy(c, to_left).wait_send()

        return 0

    lax.fori_loop(0, CHUNKS, drain, 0)
    for step in (1, 2, 3):
        q_copy(step).wait_send()
        att_copy(step).wait_send()
    part_copy.wait_send()
    mate_copy.wait_send()
    out_copy.wait_send()
    need_copy.wait_send()


def four_beams(cache, query, fresh_key_values, parents, lengths, page_table, out_weight):
    _, halves, pages, page_len, kv_width = cache.shape
    kv_heads = kv_width // HEAD_SIZE
    groups = query.shape[2] // kv_width
    chunk_shape = (CHUNKS, halves * pages * page_len // CHUNKS, kv_width)
    q_part = query.reshape(2, kv_heads, groups, HEAD_SIZE).transpose(1, 2, 0, 3)
    q_part = q_part.reshape(kv_heads, groups * 2, HEAD_SIZE)
    fresh_part = fresh_key_values.reshape(4, kv_heads, HEAD_SIZE).transpose(1, 0, 2)
    qf = jnp.concatenate(
        [q_part, jnp.pad(fresh_part, ((0, 0), (0, 12), (0, 0)))], axis=1)
    rows = 4 * 16
    out_rows, out_columns = 4, out_weight.shape[1]
    vmem = pltpu.VMEM
    half_heads = kv_heads // 2
    big = vmem(chunk_shape, jnp.bfloat16)
    dma = pltpu.SemaphoreType.DMA
    smem = pltpu.SMEM
    vmem_spec = pl.BlockSpec(memory_space=pltpu.VMEM)
    any_spec = pl.BlockSpec(memory_space=pl.ANY)
    moved, spare, second, out = pl.pallas_call(
        chain_kernel,
        out_shape=[
            jax.ShapeDtypeStruct(chunk_shape, jnp.bfloat16),
            jax.ShapeDtypeStruct(chunk_shape, jnp.bfloat16),
            jax.ShapeDtypeStruct((8, 128), jnp.int32),
            jax.ShapeDtypeStruct((out_rows, out_columns), jnp.bfloat16),
        ],
        in_specs=[any_spec, any_spec, any_spec, vmem_spec, any_spec, any_spec],
        out_specs=[any_spec, any_spec, vmem_spec, vmem_spec],
        scratch_shapes=[
            smem(parents.shape, jnp.int32), smem(lengths.shape, jnp.int32),
            smem(page_table.shape, jnp.int32),
            big, big, big, big, big, big, big,
            vmem(out_weight.shape, jnp.bfloat16),
            vmem((4, kv_heads, 32, HEAD_SIZE), jnp.bfloat16),
            vmem((kv_heads, rows, HEAD_SIZE), jnp.bfloat16),
            vmem((2, half_heads, 2, rows, HEAD_SIZE), jnp.float32),
            vmem((half_heads, 2, rows, HEAD_SIZE), jnp.float32),
            vmem((4, half_heads, rows, HEAD_SIZE), jnp.bfloat16),
            vmem((2, half_heads, rows, HEAD_SIZE), jnp.bfloat16),
            vmem((2, out_rows, out_columns), jnp.float32),
            vmem((out_rows, out_columns), jnp.float32),
            vmem((8, 128), jnp.int32),
            vmem((8, 128), jnp.int32),
            dma((3,)), dma, dma,
            dma((CHUNKS,)), dma((CHUNKS,)), dma((CHUNKS,)), dma((CHUNKS,)),
            dma((CHUNKS,)), dma((CHUNKS,)),
            dma((4,)), dma((4,)), dma((4,)), dma((4,)), dma((4,)), dma((4,)),
        ],
        compiler_params=pltpu.CompilerParams(
            collective_id=0, has_side_effects=True, vmem_limit_bytes=48 * 1024 * 1024),
        name="chain",
    )(parents, lengths, page_table, qf, cache.reshape(chunk_shape), out_weight)

    here = lax.axis_index("dp")
    low = (parents[2] < 2) & (parents[3] < 2) & (parents[2] != parents[3]) & (here == 2)
    high = (parents[0] > 1) & (parents[1] > 1) & (parents[0] != parents[1]) & (here == 1)

    def again(first, payload):
        arrived = lax.ppermute(payload, "dp", [(1, 2), (2, 1)])
        return jnp.where(low | high, arrived, first)

    moved = lax.cond(second[0, 0] > 0, again, lambda first, payload: first, moved, spare)
    return (moved.reshape(cache.shape), out)


def solution(mesh):
    in_specs = (
        P(("groups", "dp"), None, "seq", None, "tensor"),
        P(("groups", "dp"), None, "tensor"),
        P(("groups", "dp"), None, None, "tensor"),
        P("groups"),
        P("groups"),
        P("groups", None),
        P("tensor", ("dp", "seq")),
    )
    out_specs = (
        P(("groups", "dp"), None, "seq", None, "tensor"),
        P(("groups", "tensor"), ("dp", "seq")),
    )
    sizes = tuple(mesh.shape[axis] for axis in ("groups", "dp", "tensor", "seq"))
    body = four_beams if sizes == (2, 4, 2, 2) else per_device
    return jax.shard_map(
        body, mesh=mesh, in_specs=in_specs, out_specs=out_specs, check_vma=False
    )
```

```python
import math

import jax
import jax.numpy as jnp
from jax import lax
from jax.experimental import pallas as pl
from jax.experimental.pallas import tpu as pltpu
from jax.sharding import PartitionSpec as P

HEAD_SIZE = 128


NEG_FILL = -1e30


def joined(shard, axis, combine):
    everything = jax.tree.map(lambda part: lax.all_gather(part, axis), shard)
    first = jax.tree.map(lambda part: part[0], everything)

    def step(k, so_far):
        return combine(so_far, jax.tree.map(lambda part: part[k], everything))

    return lax.fori_loop(1, lax.axis_size(axis), step, first)


def merge_parts(first, second):
    max_first, total_first, weighted_first = first
    max_second, total_second, weighted_second = second
    max_joint = jnp.maximum(max_first, max_second)
    scale_first = jnp.exp(max_first - max_joint)
    scale_second = jnp.exp(max_second - max_joint)
    return (
        max_joint,
        total_first * scale_first + total_second * scale_second,
        weighted_first * scale_first[..., None] + weighted_second * scale_second[..., None],
    )


def partial_attention(stored_cache, queries, length_caps, page_rows):
    beam_count, _, local_pages, page_len, kv_width = stored_cache.shape
    kv_heads = kv_width // HEAD_SIZE
    new_count = queries.shape[1]
    query_groups = queries.shape[2] // kv_width
    slot_first = lax.axis_index("seq") * local_pages
    slot_ids = slot_first + jnp.arange(local_pages, dtype=jnp.int32)
    page_ids = jnp.arange(page_rows.shape[1], dtype=jnp.int32)
    page_num = jnp.sum(
        page_ids[None, None, :]
        * (page_rows[:, None, :] == slot_ids[None, :, None]).astype(jnp.int32),
        axis=2,
    )
    positions = (
        page_num[:, :, None] * page_len + jnp.arange(page_len, dtype=jnp.int32)[None, None, :]
    )
    in_length = (positions < length_caps[:, None, None]).reshape(beam_count, local_pages * page_len)
    allowed = in_length[:, None, None, None, :]
    cached_key_rows = stored_cache[:, 0].reshape(
        beam_count, local_pages * page_len, kv_heads, HEAD_SIZE
    )
    cached_value_rows = stored_cache[:, 1].reshape(
        beam_count, local_pages * page_len, kv_heads, HEAD_SIZE
    )
    grouped_queries = queries.reshape(beam_count, new_count, kv_heads, query_groups, HEAD_SIZE)
    scores = jnp.einsum(
        "ntkgd,nskd->ntkgs", grouped_queries, cached_key_rows, preferred_element_type=jnp.float32
    ) * (1.0 / math.sqrt(HEAD_SIZE))
    row_max = jnp.max(jnp.where(allowed, scores, NEG_FILL), axis=-1)
    weights = jnp.where(allowed, jnp.exp(scores - row_max[..., None]), 0.0)
    totals = jnp.sum(weights, axis=-1)
    weighted = jnp.einsum(
        "ntkgs,nskd->ntkgd",
        weights,
        cached_value_rows.astype(jnp.float32),
        precision=lax.Precision.HIGHEST,
    )
    return joined((row_max, totals, weighted), "seq", merge_parts)


def finish(merged, queries, new_pairs):
    row_max, totals, weighted = merged
    beam_count, new_count, q_width = queries.shape
    kv_width = new_pairs.shape[-1]
    kv_heads = kv_width // HEAD_SIZE
    query_groups = q_width // kv_width
    grouped_queries = queries.reshape(beam_count, new_count, kv_heads, query_groups, HEAD_SIZE)
    new_keys = new_pairs[:, 0].reshape(beam_count, new_count, kv_heads, HEAD_SIZE)
    new_values = new_pairs[:, 1].reshape(beam_count, new_count, kv_heads, HEAD_SIZE)
    scores = jnp.einsum(
        "ntkgd,nskd->ntkgs", grouped_queries, new_keys, preferred_element_type=jnp.float32
    ) * (1.0 / math.sqrt(HEAD_SIZE))
    causal = (
        jnp.arange(new_count, dtype=jnp.int32)[:, None]
        >= jnp.arange(new_count, dtype=jnp.int32)[None, :]
    )
    allowed = causal[None, :, None, None, :]
    joint_max = jnp.maximum(row_max, jnp.max(jnp.where(allowed, scores, NEG_FILL), axis=-1))
    old_scale = jnp.exp(row_max - joint_max)
    weights = jnp.where(allowed, jnp.exp(scores - joint_max[..., None]), 0.0)
    total_all = totals * old_scale + jnp.sum(weights, axis=-1)
    weighted_all = weighted * old_scale[..., None] + jnp.einsum(
        "ntkgs,nskd->ntkgd",
        weights,
        new_values.astype(jnp.float32),
        precision=lax.Precision.HIGHEST,
    )
    return (
        (weighted_all / total_all[..., None])
        .reshape(beam_count, new_count, q_width)
        .astype(jnp.bfloat16)
    )


def per_device(cache, query, fresh_key_values, parents, lengths, page_table, out_weight):
    beam_dev = cache.shape[0]
    device_here = lax.axis_index("dp")
    own_parents = lax.dynamic_slice_in_dim(parents, device_here * beam_dev, beam_dev)
    own_lengths = jnp.take(lengths, own_parents)
    own_tables = jnp.take(page_table, own_parents, axis=0)
    every_cache = lax.all_gather(cache, "dp", axis=0, tiled=True)
    moved = jnp.take(every_cache, own_parents, axis=0)
    merged = partial_attention(moved, query, own_lengths, own_tables)
    attended = finish(merged, query, fresh_key_values)
    head_rows = attended.reshape(beam_dev * attended.shape[1], attended.shape[2])
    terms = jnp.dot(
        lax.all_gather(head_rows, "dp", axis=0, tiled=True),
        out_weight,
        preferred_element_type=jnp.float32,
    )
    projected = lax.psum_scatter(
        terms.astype(jnp.bfloat16), "tensor", scatter_dimension=0, tiled=True
    )
    return (moved, projected)


MESH = pl.DeviceIdType.MESH
CHUNKS = 16
AHEAD = 3
END_LAG = 5
MID_LAG = 2


def chain_kernel(
    parents_in, lengths_in, tables_in, qf, cache, weight,
    moved, spare, second, out,
    parents, lengths, tables, own, from_left, from_right, to_right, to_left, moved_buf, spare_buf, held_weight,
    q_all, q_rows, part_send, part_recv, att_all, att_full, out_send, out_recv, need_send, need_recv,
    small_sem, own_sem, weight_sem, right_send, right_recv, left_send, left_recv, moved_sem, spare_sem,
    q_send_sem, q_recv_sem, att_send_sem, att_recv_sem, pair_send_sem, pair_recv_sem,
):
    me = lax.axis_index("dp")
    core = lax.axis_index("seq")
    tens = lax.axis_index("tensor")
    group = lax.axis_index("groups")
    beams = 4
    kv_heads = qf.shape[0]
    half_heads = kv_heads // 2
    rows = beams * 16
    chunk_rows, kv_width = own.shape[1:]
    page_len = 256
    local_pages = own.shape[0] * chunk_rows // (2 * page_len)
    stored = local_pages * page_len
    mate = {"seq": 1 - core}
    across = {"tensor": 1 - tens}
    other_group = {"groups": 1 - group}

    def far(step):
        return lax.rem(me + step, beams)

    right, left = {"dp": far(1)}, {"dp": far(3)}

    barrier = pltpu.get_barrier_semaphore()
    for peer in [{"dp": far(1)}, {"dp": far(2)}, {"dp": far(3)}, mate, across, other_group]:
        pl.semaphore_signal(barrier, inc=1, device_id=peer, device_id_type=MESH)

    smalls = [
        pltpu.make_async_copy(source, target, small_sem.at[i])
        for i, (source, target) in enumerate(
            [(parents_in, parents), (lengths_in, lengths), (tables_in, tables)])
    ]
    for small in smalls:
        small.start()
    load_own = pltpu.make_async_copy(cache, own, own_sem)
    load_own.start()
    load_weight = pltpu.make_async_copy(weight, held_weight, weight_sem)

    q_all[me] = qf[...]
    pl.semaphore_wait(barrier, 6)

    def q_copy(step):
        return pltpu.make_async_remote_copy(
            src_ref=qf, dst_ref=q_all.at[me], send_sem=q_send_sem.at[step],
            recv_sem=q_recv_sem.at[me], device_id={"dp": far(step)}, device_id_type=MESH)

    for step in (1, 2, 3):
        q_copy(step).start()
    def right_copy(c, source):
        return pltpu.make_async_remote_copy(
            src_ref=source.at[c], dst_ref=from_left.at[c], send_sem=right_send.at[c],
            recv_sem=right_recv.at[c], device_id=right, device_id_type=MESH)

    def left_copy(c, source):
        return pltpu.make_async_remote_copy(
            src_ref=source.at[c], dst_ref=from_right.at[c], send_sem=left_send.at[c],
            recv_sem=left_recv.at[c], device_id=left, device_id_type=MESH)

    middle = (me == 1) | (me == 2)

    def first_send(c):
        @pl.when(me == 0)
        def _():
            right_copy(c, cache).start()

        @pl.when(me == beams - 1)
        def _():
            left_copy(c, cache).start()

    for c in range(AHEAD):
        first_send(c)
    for small in smalls:
        small.wait()
    par = [parents[i] for i in range(beams)]
    mine = parents[me]
    low2, low3 = par[2] < 2, par[3] < 2
    high0, high1 = par[0] > 1, par[1] > 1
    twice = (low2 & low3 & (par[2] != par[3])) | (high0 & high1 & (par[0] != par[1]))
    first_right = jnp.where(low3, par[3], par[2])
    first_left = jnp.where(high0, par[0], par[1])
    pass_right = jnp.where(me == 1, first_right == 0, par[3] != 2)
    pass_left = jnp.where(me == 2, first_left == 3, par[0] != 1)
    spare_left = (me == 1) & (par[2] == 0)
    spare_right = (me == 2) & (par[1] == 3)
    take_left, take_right = mine < me, mine > me

    need_send[...] = jnp.full(need_send.shape, jnp.where(twice, 1, 0), jnp.int32)
    need_copy = pltpu.make_async_remote_copy(
        src_ref=need_send, dst_ref=need_recv, send_sem=pair_send_sem.at[3],
        recv_sem=pair_recv_sem.at[3], device_id=other_group, device_id_type=MESH)
    need_copy.start()

    load_own.wait()
    load_weight.start()

    ends = (me == 0) | (me == beams - 1)
    lag_right = jnp.where(me == 1, 0, jnp.where(me == 2, MID_LAG, END_LAG))
    lag_left = jnp.where(me == 2, 0, jnp.where(me == 1, MID_LAG, END_LAG))
    lag_moved = jnp.where(ends, END_LAG, MID_LAG)

    def serve(s, _):
        @pl.when(s < CHUNKS - AHEAD)
        def _():
            @pl.when(me == 0)
            def _():
                right_copy(s, cache).wait_send()

            @pl.when(me == beams - 1)
            def _():
                left_copy(s, cache).wait_send()

            first_send(s + AHEAD)

        c_right = s - lag_right
        c_left = s - lag_left

        @pl.when((me > 0) & (c_right >= 0) & (c_right < CHUNKS))
        def _():
            right_copy(c_right, to_right).wait_recv()

            @pl.when(middle)
            def _():
                to_right[c_right] = jnp.where(pass_right, from_left[c_right], own[c_right])
                right_copy(c_right, to_right).start()

        @pl.when((me < beams - 1) & (c_left >= 0) & (c_left < CHUNKS))
        def _():
            left_copy(c_left, to_left).wait_recv()

            @pl.when(middle)
            def _():
                to_left[c_left] = jnp.where(pass_left, from_right[c_left], own[c_left])
                left_copy(c_left, to_left).start()

        c = s - lag_moved

        @pl.when((c >= 0) & (c < CHUNKS))
        def _():
            moved_buf[c] = jnp.where(
                take_left, from_left[c], jnp.where(take_right, from_right[c], own[c]))
            pltpu.make_async_copy(moved_buf.at[c], moved.at[c], moved_sem.at[c]).start()

            @pl.when(middle)
            def _():
                spare_buf[c] = jnp.where(
                    spare_left, from_left[c], jnp.where(spare_right, from_right[c], own[c]))
                pltpu.make_async_copy(spare_buf.at[c], spare.at[c], spare_sem.at[c]).start()

        return 0

    def serves(lo, hi):
        lax.fori_loop(lo, hi, serve, 0)

    row_ids = lax.broadcasted_iota(jnp.int32, (rows, 1), 0)
    row_beam = lax.rem(row_ids, 2 * beams) // 2
    row_token = lax.rem(row_ids, 2)
    row_parent = jnp.zeros((rows, 1), jnp.int32)
    for i in range(beams):
        row_parent = jnp.where(row_beam == i, par[i], row_parent)
    slot_ids = lax.broadcasted_iota(jnp.int32, (1, stored), 1)
    page_base = jnp.zeros((1, stored), jnp.int32)
    for slot in range(local_pages):
        page = jnp.int32(0)
        for j in range(tables.shape[1]):
            page = page + jnp.where(tables[me, j] == core * local_pages + slot, j, 0)
        page_base = jnp.where(slot_ids // page_len == slot, page * page_len, page_base)
    allowed = page_base + lax.rem(slot_ids, page_len) < lengths[me]
    scale = 1.0 / math.sqrt(HEAD_SIZE)

    def queries_ready():
        for step in (1, 2, 3):
            pltpu.make_async_remote_copy(
                src_ref=qf, dst_ref=q_all.at[far(step)], send_sem=q_send_sem.at[step],
                recv_sem=q_recv_sem.at[far(step)], device_id={"dp": far(step)},
                device_id_type=MESH).wait_recv()
        r = lax.broadcasted_iota(jnp.int32, (rows, rows), 0)
        col = lax.broadcasted_iota(jnp.int32, (rows, rows), 1)
        place = lax.rem(r, 2 * beams) // 2 * 16 + r // (2 * beams) * 2 + lax.rem(r, 2)
        order = jnp.where(place == col, 1.0, 0.0).astype(jnp.bfloat16)
        for k in range(kv_heads):
            stacked = jnp.concatenate([q_all[i, k, 0:16, :] for i in range(beams)], axis=0)
            q_rows[k] = jnp.dot(order, stacked, preferred_element_type=jnp.float32).astype(
                jnp.bfloat16)

    half = own.shape[0] // 2

    def head(k, store, at):
        lanes = pl.ds(pl.multiple_of(k * HEAD_SIZE, HEAD_SIZE), HEAD_SIZE)
        keys = own[0:half, :, lanes].reshape(stored, HEAD_SIZE)
        values = own[half:2 * half, :, lanes].reshape(stored, HEAD_SIZE)
        scores = lax.dot_general(
            q_rows[k], keys, (((1,), (1,)), ((), ())), preferred_element_type=jnp.float32) * scale
        top = jnp.max(jnp.where(allowed, scores, NEG_FILL), axis=1, keepdims=True)
        weights = jnp.where(allowed, jnp.exp(scores - top), 0.0)
        total = jnp.sum(weights, axis=1, keepdims=True)
        coarse = weights.astype(jnp.bfloat16)
        fine = (weights - coarse.astype(jnp.float32)).astype(jnp.bfloat16)
        both = jnp.dot(
            jnp.concatenate([coarse, fine], axis=0), values, preferred_element_type=jnp.float32)
        store[at, 0] = both[:rows] + both[rows:]
        lane = lax.broadcasted_iota(jnp.int32, (rows, HEAD_SIZE), 1)
        store[at, 1] = jnp.where(lane < 1, top, total)

    part_copy = pltpu.make_async_remote_copy(
        src_ref=part_send.at[0], dst_ref=part_recv, send_sem=pair_send_sem.at[0],
        recv_sem=pair_recv_sem.at[0], device_id=mate, device_id_type=MESH)

    def spread(k, first_row):
        full = jnp.zeros((rows, HEAD_SIZE), jnp.float32)
        for i in range(beams):
            block = q_all[i, k, 16:32, :].astype(jnp.float32)[first_row:first_row + 1]
            full = jnp.where(row_beam == i, block, full)
        return full

    def att_copy(step):
        return pltpu.make_async_remote_copy(
            src_ref=att_all.at[me], dst_ref=att_all.at[me], send_sem=att_send_sem.at[step],
            recv_sem=att_recv_sem.at[me], device_id={"dp": far(step)}, device_id_type=MESH)

    def merge():
        part_copy.wait_recv()
        for at in range(half_heads):
            k = core * half_heads + at
            stat_here, stat_there = part_send[1, at, 1], part_recv[at, 1]
            top_here, top_there = stat_here[:, 0:1], stat_there[:, 0:1]
            q_here = q_rows[k].astype(jnp.float32)
            score0 = jnp.sum(q_here * spread(k, 0), axis=1, keepdims=True) * scale
            score1 = jnp.sum(q_here * spread(k, 1), axis=1, keepdims=True) * scale
            score1 = jnp.where(row_token == 1, score1, NEG_FILL)
            top = jnp.maximum(jnp.maximum(top_here, top_there), jnp.maximum(score0, score1))
            scale_here, scale_there = jnp.exp(top_here - top), jnp.exp(top_there - top)
            weight0 = jnp.exp(score0 - top)
            weight1 = jnp.where(row_token == 1, jnp.exp(score1 - top), 0.0)
            total = (stat_here[:, 1:2] * scale_here + stat_there[:, 1:2] * scale_there
                     + weight0 + weight1)
            weighted = (part_send[1, at, 0] * scale_here + part_recv[at, 0] * scale_there
                        + weight0 * spread(k, 2) + weight1 * spread(k, 3))
            att_all[me, at] = (weighted / total).astype(jnp.bfloat16)
        for step in (1, 2, 3):
            att_copy(step).start()

    mate_copy = pltpu.make_async_remote_copy(
        src_ref=att_full.at[core], dst_ref=att_full.at[core], send_sem=pair_send_sem.at[1],
        recv_sem=pair_recv_sem.at[1], device_id=mate, device_id_type=MESH)
    mate_wait = pltpu.make_async_remote_copy(
        src_ref=att_full.at[1 - core], dst_ref=att_full.at[1 - core],
        send_sem=pair_send_sem.at[1],
        recv_sem=pair_recv_sem.at[1], device_id=mate, device_id_type=MESH)

    def pick():
        for step in (1, 2, 3):
            pltpu.make_async_remote_copy(
                src_ref=att_all.at[me], dst_ref=att_all.at[far(step)],
                send_sem=att_send_sem.at[step], recv_sem=att_recv_sem.at[far(step)],
                device_id={"dp": far(step)}, device_id_type=MESH).wait_recv()
        for at in range(half_heads):
            chosen = jnp.zeros((rows, HEAD_SIZE), jnp.float32)
            for i in range(beams):
                chosen = jnp.where(row_parent == i, att_all[i, at].astype(jnp.float32), chosen)
            att_full[core, at] = chosen.astype(jnp.bfloat16)
        mate_copy.start()

    out_copy = pltpu.make_async_remote_copy(
        src_ref=out_send.at[1 - tens], dst_ref=out_recv, send_sem=pair_send_sem.at[2],
        recv_sem=pair_recv_sem.at[2], device_id=across, device_id_type=MESH)
    row_count = 2 * beams

    tile = 256
    column_tiles = held_weight.shape[1] // tile

    def flatten():
        mate_wait.wait_recv()
        load_weight.wait()
        pieces = []
        for k in range(kv_heads):
            whole = att_full[k // half_heads, k % half_heads].astype(jnp.float32)
            pieces += [whole[g * row_count:(g + 1) * row_count] for g in range(rows // row_count)]
        return jnp.concatenate(pieces, axis=1).astype(jnp.bfloat16)

    def column(flat, j):
        lanes = pl.ds(pl.multiple_of(j * tile, tile), tile)
        term = jnp.dot(flat, held_weight[:, lanes], preferred_element_type=jnp.float32)
        share = row_count // 2
        out_send[0, :, lanes] = term[:share]
        out_send[1, :, lanes] = term[share:]
        return serve(12 + j, 0)

    queries_ready()
    serves(0, 0)
    head((1 - core) * half_heads, part_send.at[0], 0)
    serves(0, 1)
    head((1 - core) * half_heads + 1, part_send.at[0], 1)
    part_copy.start()
    serves(1, 2)
    head(core * half_heads, part_send.at[1], 0)
    serves(2, 3)
    head(core * half_heads + 1, part_send.at[1], 1)
    serves(3, 4)
    merge()
    serves(4, 10)
    pick()
    serves(10, 12)
    flat = flatten()
    lax.fori_loop(0, column_tiles, lambda j, _: column(flat, j), 0)
    out_copy.start()
    serves(12 + column_tiles, CHUNKS + END_LAG)
    out_copy.wait_recv()
    out[...] = (out_send[tens] + out_recv[...]).astype(jnp.bfloat16)
    need_copy.wait_recv()
    second[...] = jnp.maximum(need_send[...], need_recv[...])

    def drain(c, _):
        pltpu.make_async_copy(moved_buf.at[c], moved.at[c], moved_sem.at[c]).wait()

        @pl.when(middle)
        def _():
            pltpu.make_async_copy(spare_buf.at[c], spare.at[c], spare_sem.at[c]).wait()

        late = (c >= CHUNKS - AHEAD)

        @pl.when(middle | ((me == 0) & late))
        def _():
            right_copy(c, to_right).wait_send()

        @pl.when(middle | ((me == beams - 1) & late))
        def _():
            left_copy(c, to_left).wait_send()

        return 0

    lax.fori_loop(0, CHUNKS, drain, 0)
    for step in (1, 2, 3):
        q_copy(step).wait_send()
        att_copy(step).wait_send()
    part_copy.wait_send()
    mate_copy.wait_send()
    out_copy.wait_send()
    need_copy.wait_send()


def four_beams(cache, query, fresh_key_values, parents, lengths, page_table, out_weight):
    _, halves, pages, page_len, kv_width = cache.shape
    kv_heads = kv_width // HEAD_SIZE
    groups = query.shape[2] // kv_width
    chunk_shape = (CHUNKS, halves * pages * page_len // CHUNKS, kv_width)
    q_part = query.reshape(2, kv_heads, groups, HEAD_SIZE).transpose(1, 2, 0, 3)
    q_part = q_part.reshape(kv_heads, groups * 2, HEAD_SIZE)
    fresh_part = fresh_key_values.reshape(4, kv_heads, HEAD_SIZE).transpose(1, 0, 2)
    qf = jnp.concatenate(
        [q_part, jnp.pad(fresh_part, ((0, 0), (0, 12), (0, 0)))], axis=1)
    rows = 4 * 16
    out_rows, out_columns = 4, out_weight.shape[1]
    vmem = pltpu.VMEM
    half_heads = kv_heads // 2
    big = vmem(chunk_shape, jnp.bfloat16)
    dma = pltpu.SemaphoreType.DMA
    smem = pltpu.SMEM
    vmem_spec = pl.BlockSpec(memory_space=pltpu.VMEM)
    any_spec = pl.BlockSpec(memory_space=pl.ANY)
    moved, spare, second, out = pl.pallas_call(
        chain_kernel,
        out_shape=[
            jax.ShapeDtypeStruct(chunk_shape, jnp.bfloat16),
            jax.ShapeDtypeStruct(chunk_shape, jnp.bfloat16),
            jax.ShapeDtypeStruct((8, 128), jnp.int32),
            jax.ShapeDtypeStruct((out_rows, out_columns), jnp.bfloat16),
        ],
        in_specs=[any_spec, any_spec, any_spec, vmem_spec, any_spec, any_spec],
        out_specs=[any_spec, any_spec, vmem_spec, vmem_spec],
        scratch_shapes=[
            smem(parents.shape, jnp.int32), smem(lengths.shape, jnp.int32),
            smem(page_table.shape, jnp.int32),
            big, big, big, big, big, big, big,
            vmem(out_weight.shape, jnp.bfloat16),
            vmem((4, kv_heads, 32, HEAD_SIZE), jnp.bfloat16),
            vmem((kv_heads, rows, HEAD_SIZE), jnp.bfloat16),
            vmem((2, half_heads, 2, rows, HEAD_SIZE), jnp.float32),
            vmem((half_heads, 2, rows, HEAD_SIZE), jnp.float32),
            vmem((4, half_heads, rows, HEAD_SIZE), jnp.bfloat16),
            vmem((2, half_heads, rows, HEAD_SIZE), jnp.bfloat16),
            vmem((2, out_rows, out_columns), jnp.float32),
            vmem((out_rows, out_columns), jnp.float32),
            vmem((8, 128), jnp.int32),
            vmem((8, 128), jnp.int32),
            dma((3,)), dma, dma,
            dma((CHUNKS,)), dma((CHUNKS,)), dma((CHUNKS,)), dma((CHUNKS,)),
            dma((CHUNKS,)), dma((CHUNKS,)),
            dma((4,)), dma((4,)), dma((4,)), dma((4,)), dma((4,)), dma((4,)),
        ],
        compiler_params=pltpu.CompilerParams(
            collective_id=0, has_side_effects=True, vmem_limit_bytes=60 * 1024 * 1024),
        name="chain",
    )(parents, lengths, page_table, qf, cache.reshape(chunk_shape), out_weight)

    here = lax.axis_index("dp")
    low = (parents[2] < 2) & (parents[3] < 2) & (parents[2] != parents[3]) & (here == 2)
    high = (parents[0] > 1) & (parents[1] > 1) & (parents[0] != parents[1]) & (here == 1)

    def again(first, payload):
        arrived = lax.ppermute(payload, "dp", [(1, 2), (2, 1)])
        return jnp.where(low | high, arrived, first)

    moved = lax.cond(second[0, 0] > 0, again, lambda first, payload: first, moved, spare)
    return (moved.reshape(cache.shape), out)


def solution(mesh):
    in_specs = (
        P(("groups", "dp"), None, "seq", None, "tensor"),
        P(("groups", "dp"), None, "tensor"),
        P(("groups", "dp"), None, None, "tensor"),
        P("groups"),
        P("groups"),
        P("groups", None),
        P("tensor", ("dp", "seq")),
    )
    out_specs = (
        P(("groups", "dp"), None, "seq", None, "tensor"),
        P(("groups", "tensor"), ("dp", "seq")),
    )
    sizes = tuple(mesh.shape[axis] for axis in ("groups", "dp", "tensor", "seq"))
    body = four_beams if sizes == (2, 4, 2, 2) else per_device
    return jax.shard_map(
        body, mesh=mesh, in_specs=in_specs, out_specs=out_specs, check_vma=False
    )
```

```python
import math

import jax
import jax.numpy as jnp
from jax import lax
from jax.experimental import pallas as pl
from jax.experimental.pallas import tpu as pltpu
from jax.sharding import PartitionSpec as P

HEAD_SIZE = 128


NEG_FILL = -1e30


def joined(shard, axis, combine):
    everything = jax.tree.map(lambda part: lax.all_gather(part, axis), shard)
    first = jax.tree.map(lambda part: part[0], everything)

    def step(k, so_far):
        return combine(so_far, jax.tree.map(lambda part: part[k], everything))

    return lax.fori_loop(1, lax.axis_size(axis), step, first)


def merge_parts(first, second):
    max_first, total_first, weighted_first = first
    max_second, total_second, weighted_second = second
    max_joint = jnp.maximum(max_first, max_second)
    scale_first = jnp.exp(max_first - max_joint)
    scale_second = jnp.exp(max_second - max_joint)
    return (
        max_joint,
        total_first * scale_first + total_second * scale_second,
        weighted_first * scale_first[..., None] + weighted_second * scale_second[..., None],
    )


def partial_attention(stored_cache, queries, length_caps, page_rows):
    beam_count, _, local_pages, page_len, kv_width = stored_cache.shape
    kv_heads = kv_width // HEAD_SIZE
    new_count = queries.shape[1]
    query_groups = queries.shape[2] // kv_width
    slot_first = lax.axis_index("seq") * local_pages
    slot_ids = slot_first + jnp.arange(local_pages, dtype=jnp.int32)
    page_ids = jnp.arange(page_rows.shape[1], dtype=jnp.int32)
    page_num = jnp.sum(
        page_ids[None, None, :]
        * (page_rows[:, None, :] == slot_ids[None, :, None]).astype(jnp.int32),
        axis=2,
    )
    positions = (
        page_num[:, :, None] * page_len + jnp.arange(page_len, dtype=jnp.int32)[None, None, :]
    )
    in_length = (positions < length_caps[:, None, None]).reshape(beam_count, local_pages * page_len)
    allowed = in_length[:, None, None, None, :]
    cached_key_rows = stored_cache[:, 0].reshape(
        beam_count, local_pages * page_len, kv_heads, HEAD_SIZE
    )
    cached_value_rows = stored_cache[:, 1].reshape(
        beam_count, local_pages * page_len, kv_heads, HEAD_SIZE
    )
    grouped_queries = queries.reshape(beam_count, new_count, kv_heads, query_groups, HEAD_SIZE)
    scores = jnp.einsum(
        "ntkgd,nskd->ntkgs", grouped_queries, cached_key_rows, preferred_element_type=jnp.float32
    ) * (1.0 / math.sqrt(HEAD_SIZE))
    row_max = jnp.max(jnp.where(allowed, scores, NEG_FILL), axis=-1)
    weights = jnp.where(allowed, jnp.exp(scores - row_max[..., None]), 0.0)
    totals = jnp.sum(weights, axis=-1)
    weighted = jnp.einsum(
        "ntkgs,nskd->ntkgd",
        weights,
        cached_value_rows.astype(jnp.float32),
        precision=lax.Precision.HIGHEST,
    )
    return joined((row_max, totals, weighted), "seq", merge_parts)


def finish(merged, queries, new_pairs):
    row_max, totals, weighted = merged
    beam_count, new_count, q_width = queries.shape
    kv_width = new_pairs.shape[-1]
    kv_heads = kv_width // HEAD_SIZE
    query_groups = q_width // kv_width
    grouped_queries = queries.reshape(beam_count, new_count, kv_heads, query_groups, HEAD_SIZE)
    new_keys = new_pairs[:, 0].reshape(beam_count, new_count, kv_heads, HEAD_SIZE)
    new_values = new_pairs[:, 1].reshape(beam_count, new_count, kv_heads, HEAD_SIZE)
    scores = jnp.einsum(
        "ntkgd,nskd->ntkgs", grouped_queries, new_keys, preferred_element_type=jnp.float32
    ) * (1.0 / math.sqrt(HEAD_SIZE))
    causal = (
        jnp.arange(new_count, dtype=jnp.int32)[:, None]
        >= jnp.arange(new_count, dtype=jnp.int32)[None, :]
    )
    allowed = causal[None, :, None, None, :]
    joint_max = jnp.maximum(row_max, jnp.max(jnp.where(allowed, scores, NEG_FILL), axis=-1))
    old_scale = jnp.exp(row_max - joint_max)
    weights = jnp.where(allowed, jnp.exp(scores - joint_max[..., None]), 0.0)
    total_all = totals * old_scale + jnp.sum(weights, axis=-1)
    weighted_all = weighted * old_scale[..., None] + jnp.einsum(
        "ntkgs,nskd->ntkgd",
        weights,
        new_values.astype(jnp.float32),
        precision=lax.Precision.HIGHEST,
    )
    return (
        (weighted_all / total_all[..., None])
        .reshape(beam_count, new_count, q_width)
        .astype(jnp.bfloat16)
    )


def per_device(cache, query, fresh_key_values, parents, lengths, page_table, out_weight):
    beam_dev = cache.shape[0]
    device_here = lax.axis_index("dp")
    own_parents = lax.dynamic_slice_in_dim(parents, device_here * beam_dev, beam_dev)
    own_lengths = jnp.take(lengths, own_parents)
    own_tables = jnp.take(page_table, own_parents, axis=0)
    every_cache = lax.all_gather(cache, "dp", axis=0, tiled=True)
    moved = jnp.take(every_cache, own_parents, axis=0)
    merged = partial_attention(moved, query, own_lengths, own_tables)
    attended = finish(merged, query, fresh_key_values)
    head_rows = attended.reshape(beam_dev * attended.shape[1], attended.shape[2])
    terms = jnp.dot(
        lax.all_gather(head_rows, "dp", axis=0, tiled=True),
        out_weight,
        preferred_element_type=jnp.float32,
    )
    projected = lax.psum_scatter(
        terms.astype(jnp.bfloat16), "tensor", scatter_dimension=0, tiled=True
    )
    return (moved, projected)


MESH = pl.DeviceIdType.MESH
CHUNKS = 16
AHEAD = 3
END_LAG = 5
MID_LAG = 2


def chain_kernel(
    parents_in, lengths_in, tables_in, qf, cache, weight,
    moved, spare, second, out,
    parents, lengths, tables, own, from_left, from_right, to_right, to_left, moved_buf, spare_buf, held_weight,
    q_all, q_rows, part_send, part_recv, att_all, att_full, out_send, out_recv, need_send, need_recv,
    small_sem, own_sem, weight_sem, right_send, right_recv, left_send, left_recv, moved_sem, spare_sem,
    q_send_sem, q_recv_sem, att_send_sem, att_recv_sem, pair_send_sem, pair_recv_sem,
):
    me = lax.axis_index("dp")
    core = lax.axis_index("seq")
    tens = lax.axis_index("tensor")
    group = lax.axis_index("groups")
    beams = 4
    kv_heads = qf.shape[0]
    half_heads = kv_heads // 2
    rows = beams * 16
    chunk_rows, kv_width = own.shape[1:]
    page_len = 256
    local_pages = own.shape[0] * chunk_rows // (2 * page_len)
    stored = local_pages * page_len
    mate = {"seq": 1 - core}
    across = {"tensor": 1 - tens}
    other_group = {"groups": 1 - group}

    def far(step):
        return lax.rem(me + step, beams)

    right, left = {"dp": far(1)}, {"dp": far(3)}

    barrier = pltpu.get_barrier_semaphore()
    for peer in [{"dp": far(1)}, {"dp": far(2)}, {"dp": far(3)}, mate, across, other_group]:
        pl.semaphore_signal(barrier, inc=1, device_id=peer, device_id_type=MESH)

    smalls = [
        pltpu.make_async_copy(source, target, small_sem.at[i])
        for i, (source, target) in enumerate(
            [(parents_in, parents), (lengths_in, lengths), (tables_in, tables)])
    ]
    for small in smalls:
        small.start()
    load_own = pltpu.make_async_copy(cache, own, own_sem)
    load_own.start()
    load_weight = pltpu.make_async_copy(weight, held_weight, weight_sem)

    q_all[me] = qf[...]
    pl.semaphore_wait(barrier, 6)

    def q_copy(step):
        return pltpu.make_async_remote_copy(
            src_ref=qf, dst_ref=q_all.at[me], send_sem=q_send_sem.at[step],
            recv_sem=q_recv_sem.at[me], device_id={"dp": far(step)}, device_id_type=MESH)

    for step in (1, 2, 3):
        q_copy(step).start()
    def right_copy(c, source):
        return pltpu.make_async_remote_copy(
            src_ref=source.at[c], dst_ref=from_left.at[c], send_sem=right_send.at[c],
            recv_sem=right_recv.at[c], device_id=right, device_id_type=MESH)

    def left_copy(c, source):
        return pltpu.make_async_remote_copy(
            src_ref=source.at[c], dst_ref=from_right.at[c], send_sem=left_send.at[c],
            recv_sem=left_recv.at[c], device_id=left, device_id_type=MESH)

    middle = (me == 1) | (me == 2)

    def first_send(c):
        @pl.when(me == 0)
        def _():
            right_copy(c, cache).start()

        @pl.when(me == beams - 1)
        def _():
            left_copy(c, cache).start()

    for c in range(AHEAD):
        first_send(c)
    for small in smalls:
        small.wait()
    par = [parents[i] for i in range(beams)]
    mine = parents[me]
    low2, low3 = par[2] < 2, par[3] < 2
    high0, high1 = par[0] > 1, par[1] > 1
    twice = (low2 & low3 & (par[2] != par[3])) | (high0 & high1 & (par[0] != par[1]))
    first_right = jnp.where(low3, par[3], par[2])
    first_left = jnp.where(high0, par[0], par[1])
    pass_right = jnp.where(me == 1, first_right == 0, par[3] != 2)
    pass_left = jnp.where(me == 2, first_left == 3, par[0] != 1)
    spare_left = (me == 1) & (par[2] == 0)
    spare_right = (me == 2) & (par[1] == 3)
    take_left, take_right = mine < me, mine > me

    need_send[...] = jnp.full(need_send.shape, jnp.where(twice, 1, 0), jnp.int32)
    need_copy = pltpu.make_async_remote_copy(
        src_ref=need_send, dst_ref=need_recv, send_sem=pair_send_sem.at[3],
        recv_sem=pair_recv_sem.at[3], device_id=other_group, device_id_type=MESH)
    need_copy.start()

    load_own.wait()
    load_weight.start()

    ends = (me == 0) | (me == beams - 1)
    lag_right = jnp.where(me == 1, 0, jnp.where(me == 2, MID_LAG, END_LAG))
    lag_left = jnp.where(me == 2, 0, jnp.where(me == 1, MID_LAG, END_LAG))
    lag_moved = jnp.where(ends, END_LAG, MID_LAG)

    def serve(s, _):
        @pl.when(s < CHUNKS - AHEAD)
        def _():
            @pl.when(me == 0)
            def _():
                right_copy(s, cache).wait_send()

            @pl.when(me == beams - 1)
            def _():
                left_copy(s, cache).wait_send()

            first_send(s + AHEAD)

        c_right = s - lag_right
        c_left = s - lag_left

        @pl.when((me > 0) & (c_right >= 0) & (c_right < CHUNKS))
        def _():
            right_copy(c_right, to_right).wait_recv()

            @pl.when(middle)
            def _():
                to_right[c_right] = jnp.where(pass_right, from_left[c_right], own[c_right])
                right_copy(c_right, to_right).start()

        @pl.when((me < beams - 1) & (c_left >= 0) & (c_left < CHUNKS))
        def _():
            left_copy(c_left, to_left).wait_recv()

            @pl.when(middle)
            def _():
                to_left[c_left] = jnp.where(pass_left, from_right[c_left], own[c_left])
                left_copy(c_left, to_left).start()

        c = s - lag_moved

        @pl.when((c >= 0) & (c < CHUNKS))
        def _():
            moved_buf[c] = jnp.where(
                take_left, from_left[c], jnp.where(take_right, from_right[c], own[c]))
            pltpu.make_async_copy(moved_buf.at[c], moved.at[c], moved_sem.at[c]).start()

            @pl.when(middle)
            def _():
                spare_buf[c] = jnp.where(
                    spare_left, from_left[c], jnp.where(spare_right, from_right[c], own[c]))
                pltpu.make_async_copy(spare_buf.at[c], spare.at[c], spare_sem.at[c]).start()

        return 0

    def serves(lo, hi):
        lax.fori_loop(lo, hi, serve, 0)

    row_ids = lax.broadcasted_iota(jnp.int32, (rows, 1), 0)
    row_beam = lax.rem(row_ids, 2 * beams) // 2
    row_token = lax.rem(row_ids, 2)
    row_parent = jnp.zeros((rows, 1), jnp.int32)
    for i in range(beams):
        row_parent = jnp.where(row_beam == i, par[i], row_parent)
    slot_ids = lax.broadcasted_iota(jnp.int32, (1, stored), 1)
    page_base = jnp.zeros((1, stored), jnp.int32)
    for slot in range(local_pages):
        page = jnp.int32(0)
        for j in range(tables.shape[1]):
            page = page + jnp.where(tables[me, j] == core * local_pages + slot, j, 0)
        page_base = jnp.where(slot_ids // page_len == slot, page * page_len, page_base)
    allowed = page_base + lax.rem(slot_ids, page_len) < lengths[me]
    scale = 1.0 / math.sqrt(HEAD_SIZE)

    def queries_ready():
        for step in (1, 2, 3):
            pltpu.make_async_remote_copy(
                src_ref=qf, dst_ref=q_all.at[far(step)], send_sem=q_send_sem.at[step],
                recv_sem=q_recv_sem.at[far(step)], device_id={"dp": far(step)},
                device_id_type=MESH).wait_recv()
        r = lax.broadcasted_iota(jnp.int32, (rows, rows), 0)
        col = lax.broadcasted_iota(jnp.int32, (rows, rows), 1)
        place = lax.rem(r, 2 * beams) // 2 * 16 + r // (2 * beams) * 2 + lax.rem(r, 2)
        order = jnp.where(place == col, 1.0, 0.0).astype(jnp.bfloat16)
        for k in range(kv_heads):
            stacked = jnp.concatenate([q_all[i, k, 0:16, :] for i in range(beams)], axis=0)
            q_rows[k] = jnp.dot(order, stacked, preferred_element_type=jnp.float32).astype(
                jnp.bfloat16)

    half = own.shape[0] // 2

    def head(k, store, at):
        lanes = pl.ds(pl.multiple_of(k * HEAD_SIZE, HEAD_SIZE), HEAD_SIZE)
        keys = own[0:half, :, lanes].reshape(stored, HEAD_SIZE)
        values = own[half:2 * half, :, lanes].reshape(stored, HEAD_SIZE)
        scores = lax.dot_general(
            q_rows[k], keys, (((1,), (1,)), ((), ())), preferred_element_type=jnp.float32) * scale
        top = jnp.max(jnp.where(allowed, scores, NEG_FILL), axis=1, keepdims=True)
        weights = jnp.where(allowed, jnp.exp(scores - top), 0.0)
        total = jnp.sum(weights, axis=1, keepdims=True)
        coarse = weights.astype(jnp.bfloat16)
        fine = (weights - coarse.astype(jnp.float32)).astype(jnp.bfloat16)
        both = jnp.dot(
            jnp.concatenate([coarse, fine], axis=0), values, preferred_element_type=jnp.float32)
        store[at, 0] = both[:rows] + both[rows:]
        lane = lax.broadcasted_iota(jnp.int32, (rows, HEAD_SIZE), 1)
        store[at, 1] = jnp.where(lane < 1, top, total)

    part_copy = pltpu.make_async_remote_copy(
        src_ref=part_send.at[0], dst_ref=part_recv, send_sem=pair_send_sem.at[0],
        recv_sem=pair_recv_sem.at[0], device_id=mate, device_id_type=MESH)

    def spread(k, first_row):
        full = jnp.zeros((rows, HEAD_SIZE), jnp.float32)
        for i in range(beams):
            block = q_all[i, k, 16:32, :].astype(jnp.float32)[first_row:first_row + 1]
            full = jnp.where(row_beam == i, block, full)
        return full

    def att_copy(step):
        return pltpu.make_async_remote_copy(
            src_ref=att_all.at[me], dst_ref=att_all.at[me], send_sem=att_send_sem.at[step],
            recv_sem=att_recv_sem.at[me], device_id={"dp": far(step)}, device_id_type=MESH)

    def merge():
        part_copy.wait_recv()
        for at in range(half_heads):
            k = core * half_heads + at
            stat_here, stat_there = part_send[1, at, 1], part_recv[at, 1]
            top_here, top_there = stat_here[:, 0:1], stat_there[:, 0:1]
            q_here = q_rows[k].astype(jnp.float32)
            score0 = jnp.sum(q_here * spread(k, 0), axis=1, keepdims=True) * scale
            score1 = jnp.sum(q_here * spread(k, 1), axis=1, keepdims=True) * scale
            score1 = jnp.where(row_token == 1, score1, NEG_FILL)
            top = jnp.maximum(jnp.maximum(top_here, top_there), jnp.maximum(score0, score1))
            scale_here, scale_there = jnp.exp(top_here - top), jnp.exp(top_there - top)
            weight0 = jnp.exp(score0 - top)
            weight1 = jnp.where(row_token == 1, jnp.exp(score1 - top), 0.0)
            total = (stat_here[:, 1:2] * scale_here + stat_there[:, 1:2] * scale_there
                     + weight0 + weight1)
            weighted = (part_send[1, at, 0] * scale_here + part_recv[at, 0] * scale_there
                        + weight0 * spread(k, 2) + weight1 * spread(k, 3))
            att_all[me, at] = (weighted / total).astype(jnp.bfloat16)
        for step in (1, 2, 3):
            att_copy(step).start()

    mate_copy = pltpu.make_async_remote_copy(
        src_ref=att_full.at[core], dst_ref=att_full.at[core], send_sem=pair_send_sem.at[1],
        recv_sem=pair_recv_sem.at[1], device_id=mate, device_id_type=MESH)
    mate_wait = pltpu.make_async_remote_copy(
        src_ref=att_full.at[1 - core], dst_ref=att_full.at[1 - core],
        send_sem=pair_send_sem.at[1],
        recv_sem=pair_recv_sem.at[1], device_id=mate, device_id_type=MESH)

    def pick():
        for step in (1, 2, 3):
            pltpu.make_async_remote_copy(
                src_ref=att_all.at[me], dst_ref=att_all.at[far(step)],
                send_sem=att_send_sem.at[step], recv_sem=att_recv_sem.at[far(step)],
                device_id={"dp": far(step)}, device_id_type=MESH).wait_recv()
        for at in range(half_heads):
            chosen = jnp.zeros((rows, HEAD_SIZE), jnp.float32)
            for i in range(beams):
                chosen = jnp.where(row_parent == i, att_all[i, at].astype(jnp.float32), chosen)
            att_full[core, at] = chosen.astype(jnp.bfloat16)
        mate_copy.start()

    out_copy = pltpu.make_async_remote_copy(
        src_ref=out_send.at[1 - tens], dst_ref=out_recv, send_sem=pair_send_sem.at[2],
        recv_sem=pair_recv_sem.at[2], device_id=across, device_id_type=MESH)
    row_count = 2 * beams

    tile = 256
    column_tiles = held_weight.shape[1] // tile

    def flatten():
        mate_wait.wait_recv()
        load_weight.wait()
        pieces = []
        for k in range(kv_heads):
            whole = att_full[k // half_heads, k % half_heads].astype(jnp.float32)
            pieces += [whole[g * row_count:(g + 1) * row_count] for g in range(rows // row_count)]
        return jnp.concatenate(pieces, axis=1).astype(jnp.bfloat16)

    def column(flat, j):
        lanes = pl.ds(pl.multiple_of(j * tile, tile), tile)
        term = jnp.dot(flat, held_weight[:, lanes], preferred_element_type=jnp.float32)
        share = row_count // 2
        out_send[0, :, lanes] = term[:share]
        out_send[1, :, lanes] = term[share:]
        return serve(12 + j, 0)

    queries_ready()
    serves(0, 1)
    head((1 - core) * half_heads, part_send.at[0], 0)
    serves(1, 2)
    head((1 - core) * half_heads + 1, part_send.at[0], 1)
    part_copy.start()
    serves(2, 3)
    head(core * half_heads, part_send.at[1], 0)
    serves(3, 4)
    head(core * half_heads + 1, part_send.at[1], 1)
    serves(4, 5)
    merge()
    serves(5, 10)
    pick()
    serves(10, 12)
    flat = flatten()
    lax.fori_loop(0, column_tiles, lambda j, _: column(flat, j), 0)
    out_copy.start()
    serves(12 + column_tiles, CHUNKS + END_LAG)
    out_copy.wait_recv()
    out[...] = (out_send[tens] + out_recv[...]).astype(jnp.bfloat16)
    need_copy.wait_recv()
    second[...] = jnp.maximum(need_send[...], need_recv[...])

    def drain(c, _):
        pltpu.make_async_copy(moved_buf.at[c], moved.at[c], moved_sem.at[c]).wait()

        @pl.when(middle)
        def _():
            pltpu.make_async_copy(spare_buf.at[c], spare.at[c], spare_sem.at[c]).wait()

        late = (c >= CHUNKS - AHEAD)

        @pl.when(middle | ((me == 0) & late))
        def _():
            right_copy(c, to_right).wait_send()

        @pl.when(middle | ((me == beams - 1) & late))
        def _():
            left_copy(c, to_left).wait_send()

        return 0

    lax.fori_loop(0, CHUNKS, drain, 0)
    for step in (1, 2, 3):
        q_copy(step).wait_send()
        att_copy(step).wait_send()
    part_copy.wait_send()
    mate_copy.wait_send()
    out_copy.wait_send()
    need_copy.wait_send()


def four_beams(cache, query, fresh_key_values, parents, lengths, page_table, out_weight):
    _, halves, pages, page_len, kv_width = cache.shape
    kv_heads = kv_width // HEAD_SIZE
    groups = query.shape[2] // kv_width
    chunk_shape = (CHUNKS, halves * pages * page_len // CHUNKS, kv_width)
    q_part = query.reshape(2, kv_heads, groups, HEAD_SIZE).transpose(1, 2, 0, 3)
    q_part = q_part.reshape(kv_heads, groups * 2, HEAD_SIZE)
    fresh_part = fresh_key_values.reshape(4, kv_heads, HEAD_SIZE).transpose(1, 0, 2)
    qf = jnp.concatenate(
        [q_part, jnp.pad(fresh_part, ((0, 0), (0, 12), (0, 0)))], axis=1)
    rows = 4 * 16
    out_rows, out_columns = 4, out_weight.shape[1]
    vmem = pltpu.VMEM
    half_heads = kv_heads // 2
    big = vmem(chunk_shape, jnp.bfloat16)
    dma = pltpu.SemaphoreType.DMA
    smem = pltpu.SMEM
    vmem_spec = pl.BlockSpec(memory_space=pltpu.VMEM)
    any_spec = pl.BlockSpec(memory_space=pl.ANY)
    moved, spare, second, out = pl.pallas_call(
        chain_kernel,
        out_shape=[
            jax.ShapeDtypeStruct(chunk_shape, jnp.bfloat16),
            jax.ShapeDtypeStruct(chunk_shape, jnp.bfloat16),
            jax.ShapeDtypeStruct((8, 128), jnp.int32),
            jax.ShapeDtypeStruct((out_rows, out_columns), jnp.bfloat16),
        ],
        in_specs=[any_spec, any_spec, any_spec, vmem_spec, any_spec, any_spec],
        out_specs=[any_spec, any_spec, vmem_spec, vmem_spec],
        scratch_shapes=[
            smem(parents.shape, jnp.int32), smem(lengths.shape, jnp.int32),
            smem(page_table.shape, jnp.int32),
            big, big, big, big, big, big, big,
            vmem(out_weight.shape, jnp.bfloat16),
            vmem((4, kv_heads, 32, HEAD_SIZE), jnp.bfloat16),
            vmem((kv_heads, rows, HEAD_SIZE), jnp.bfloat16),
            vmem((2, half_heads, 2, rows, HEAD_SIZE), jnp.float32),
            vmem((half_heads, 2, rows, HEAD_SIZE), jnp.float32),
            vmem((4, half_heads, rows, HEAD_SIZE), jnp.bfloat16),
            vmem((2, half_heads, rows, HEAD_SIZE), jnp.bfloat16),
            vmem((2, out_rows, out_columns), jnp.float32),
            vmem((out_rows, out_columns), jnp.float32),
            vmem((8, 128), jnp.int32),
            vmem((8, 128), jnp.int32),
            dma((3,)), dma, dma,
            dma((CHUNKS,)), dma((CHUNKS,)), dma((CHUNKS,)), dma((CHUNKS,)),
            dma((CHUNKS,)), dma((CHUNKS,)),
            dma((4,)), dma((4,)), dma((4,)), dma((4,)), dma((4,)), dma((4,)),
        ],
        compiler_params=pltpu.CompilerParams(
            collective_id=0, has_side_effects=True, vmem_limit_bytes=60 * 1024 * 1024),
        name="chain",
    )(parents, lengths, page_table, qf, cache.reshape(chunk_shape), out_weight)

    here = lax.axis_index("dp")
    low = (parents[2] < 2) & (parents[3] < 2) & (parents[2] != parents[3]) & (here == 2)
    high = (parents[0] > 1) & (parents[1] > 1) & (parents[0] != parents[1]) & (here == 1)

    def again(first, payload):
        arrived = lax.ppermute(payload, "dp", [(1, 2), (2, 1)])
        return jnp.where(low | high, arrived, first)

    moved = lax.cond(second[0, 0] > 0, again, lambda first, payload: first, moved, spare)
    return (moved.reshape(cache.shape), out)


def solution(mesh):
    in_specs = (
        P(("groups", "dp"), None, "seq", None, "tensor"),
        P(("groups", "dp"), None, "tensor"),
        P(("groups", "dp"), None, None, "tensor"),
        P("groups"),
        P("groups"),
        P("groups", None),
        P("tensor", ("dp", "seq")),
    )
    out_specs = (
        P(("groups", "dp"), None, "seq", None, "tensor"),
        P(("groups", "tensor"), ("dp", "seq")),
    )
    sizes = tuple(mesh.shape[axis] for axis in ("groups", "dp", "tensor", "seq"))
    body = four_beams if sizes == (2, 4, 2, 2) else per_device
    return jax.shard_map(
        body, mesh=mesh, in_specs=in_specs, out_specs=out_specs, check_vma=False
    )
```
